256 devices in a mesh: seq: 16 (over y, x), asset: 16 (over z, core).
Axes of the slice: x: 4, y: 4, z: 8, core: 2. Of those that a mesh axis runs over, the one named last changes fastest.
Arguments:
- tokens: bfloat16 [16, 8192, 1024], P('asset', 'seq'), may hold values from -6 to 6
- w_query: bfloat16 [1024, 1024], replicated, may hold values from -0.1875 to 0.1875
- w_key: bfloat16 [1024, 1024], replicated, may hold values from -0.1875 to 0.1875
- w_value: bfloat16 [1024, 1024], replicated, may hold values from -0.1875 to 0.1875
- decay_log: float32 [16, 8, 8192], P('asset', None, 'seq'), may hold values from -1 to 0, as said below
- lengths: int32 [16], P('asset'), may hold values from 128 to 8192, as said below
- sources: int32 [16], replicated, may hold values from 0 to 15, as said below
- targets: int32 [16], replicated, may hold values from 0 to 15, as said below
- stash: float32 [16, 8, 128, 128], P('asset', None, 'seq'), may hold values from -24 to 24
- whiten: bfloat16 [16, 1024, 1024], P('asset'), may hold values from -0.1875 to 0.1875
Outputs:
- features: bfloat16 [16, 8192, 1024], P('asset', 'seq')
- kept_states: float32 [16, 8, 128, 128], P('asset', None, 'seq')
The draws below stay inside these ranges and needn't reach their ends.
Inputs may be any that keep to these rules, and one draw needn't show every extreme that they name: `decay_log`: negative. `lengths`: multiples of 128; some asset has 8192 valid steps and another 128. `sources`: a permutation of the asset numbers. `targets`: a permutation of the asset numbers.
All inputs are finite; a program needn't handle non-finite values.
Results may differ from the reference program's by a relative error of at most 0.0067.
Values sent between devices are 32-bit elements; how exact they have to be, the bound alone decides.
No kernel may reach another device: no remote copies, remote signals or barrier semaphores. Data moves between devices by JAX's collectives and lax.ppermute only.
A program may use at most 128 MiB of HBM per device.

```python
import math
import jax
import jax.numpy as jnp
from jax import lax

D = 1024
RETENTION_HEADS = 8
HEAD_DIM = 128
SPAN = 128
A_DEV = 1
ASSET_TOTAL = 16
STREAM_LENGTH = 8192


def draw_decay_log(key, part):
    fast_key, block_key, rough_key, position_key, dropout_key = jax.random.split(key, 5)
    fast_share = 5
    blocks = STREAM_LENGTH // SPAN
    fast_heads = jax.random.randint(fast_key, (ASSET_TOTAL, RETENTION_HEADS, 1, 1), 0, 10) < fast_share
    base_rate = jnp.where(fast_heads, 1.0 / 40.0, 0.5 / STREAM_LENGTH)
    block_factor = jnp.exp(jax.random.uniform(block_key, (ASSET_TOTAL, RETENTION_HEADS, blocks, 1), jnp.float32, -math.log(2.0), math.log(2.0)))
    roughness = jax.random.uniform(rough_key, (ASSET_TOTAL, RETENTION_HEADS, blocks, SPAN), jnp.float32, 0.5, 1.5)
    forget_factor = (base_rate * block_factor * roughness).reshape(ASSET_TOTAL, RETENTION_HEADS, STREAM_LENGTH)
    spike_positions = jax.random.randint(position_key, (ASSET_TOTAL, RETENTION_HEADS, 2, 1), 0, STREAM_LENGTH)
    spike_magnitudes = jax.random.uniform(dropout_key, (ASSET_TOTAL, RETENTION_HEADS, 2, 1), jnp.float32, math.log(0.5), math.log(0.8))
    step_indices = jnp.arange(STREAM_LENGTH, dtype=jnp.int32)
    spike_events = jnp.sum(jnp.where(spike_positions == step_indices, spike_magnitudes, 0.0), axis=2)
    return (spike_events - forget_factor).astype(jnp.float32)


def draw_lengths(key, part):
    count_key, full_key, short_key = jax.random.split(key, 3)
    blocks = STREAM_LENGTH // SPAN
    counts = jax.random.randint(count_key, (ASSET_TOTAL,), 1, blocks + 1)
    full_asset = jax.random.randint(full_key, (), 0, ASSET_TOTAL)
    short_asset = (full_asset + jax.random.randint(short_key, (), 1, ASSET_TOTAL)) % ASSET_TOTAL
    numbers = jnp.arange(ASSET_TOTAL, dtype=jnp.int32)
    counts = jnp.where(numbers == full_asset, blocks, jnp.where(numbers == short_asset, 1, counts))
    return (counts * SPAN).astype(jnp.int32)


def force_pair(order, numbers, asset, slot):
    holder = jnp.argmax(order == slot).astype(jnp.int32)
    previous = order[asset]
    moved = jnp.where(numbers == holder, previous, order)
    moved = jnp.where(numbers == asset, slot, moved)
    return moved.astype(jnp.int32)


def slot_route(key):
    order_key, chosen_key = jax.random.split(key, 2)
    numbers = jnp.arange(ASSET_TOTAL, dtype=jnp.int32)
    shuffled = jax.random.permutation(order_key, numbers).astype(jnp.int32)
    chosen = jax.random.randint(chosen_key, (), 0, ASSET_TOTAL).astype(jnp.int32)
    far_slot = ((chosen + ASSET_TOTAL // 2) % ASSET_TOTAL).astype(jnp.int32)
    routed = force_pair(shuffled, numbers, chosen, far_slot)
    second = far_slot
    next_slot = ((second + A_DEV) % ASSET_TOTAL).astype(jnp.int32)
    routed = force_pair(routed, numbers, second, next_slot)
    return routed.astype(jnp.int32)


def draw_sources(key, part):
    return slot_route(jax.random.fold_in(key, 71))


def draw_targets(key, part):
    return slot_route(jax.random.fold_in(key, 137))


def level_of(key, extent, pieces, low, top_value):
    factor_of = 1.0
    for position, shards_of in pieces:
        draws = jax.random.uniform(jax.random.fold_in(jax.random.fold_in(key, 6), position), (shards_of,), jnp.float32, low / len(pieces), top_value / len(pieces))
        factor_of = factor_of * jnp.repeat(jnp.exp(draws), extent[position] // shards_of).reshape((-1,) + (1,) * (len(extent) - 1 - position))
    return factor_of


def bell_draw(rng, shape, deviation, limit, shards=(), held_as=jnp.bfloat16):
    entries = jax.random.normal(rng, shape, jnp.float32) * deviation
    if len(shards) > 0:
        entries = level_of(rng, shape, shards, -0.22, 0.18) * entries
    return jnp.clip(entries, min=-limit, max=limit).astype(held_as)


def setup_inputs(seed: int = 0) -> dict:
    seeds = jax.random.split(jax.random.key(seed), 11)
    tokens = bell_draw(seeds[0], (ASSET_TOTAL, STREAM_LENGTH, D), 1.0, 6.0, ((0, 16), (1, 16)))
    w_query = bell_draw(seeds[1], (D, D), D ** -0.5, 0.1875)
    w_key = bell_draw(seeds[2], (D, D), D ** -0.5, 0.1875)
    w_value = bell_draw(seeds[3], (D, D), D ** -0.5, 0.1875)
    decay_log = draw_decay_log(jax.random.fold_in(seeds[10], 71), 0)
    lengths = draw_lengths(jax.random.fold_in(seeds[10], 71), 0)
    sources = draw_sources(jax.random.fold_in(seeds[10], 71), 0)
    targets = draw_targets(jax.random.fold_in(seeds[10], 71), 0)
    stash = bell_draw(seeds[8], (ASSET_TOTAL, RETENTION_HEADS, HEAD_DIM, HEAD_DIM), 4.0, 24.0, ((0, 16), (2, 16)), jnp.float32)
    whiten = bell_draw(seeds[9], (ASSET_TOTAL, D, D), D ** -0.5, 0.1875, ((0, 16),))
    return {"tokens": tokens, "w_query": w_query, "w_key": w_key, "w_value": w_value, "decay_log": decay_log, "lengths": lengths, "sources": sources, "targets": targets, "stash": stash, "whiten": whiten}


HIGHEST_PRECISION = lax.Precision.HIGHEST
EPSILON = 1e-05

def rounded(values):
    return lax.optimization_barrier(values.astype(jnp.bfloat16)).astype(jnp.float32)

def one_asset(tokens, decay_log, length, start_state, whiten, w_query, w_key, w_value):
    key_scale = HEAD_DIM ** (-0.5)
    queries = jnp.dot(tokens, w_query, preferred_element_type=jnp.float32).astype(jnp.bfloat16)
    key_rows = (jnp.dot(tokens, w_key, preferred_element_type=jnp.float32) * key_scale).astype(jnp.bfloat16)
    value_rows = jnp.dot(tokens, w_value, preferred_element_type=jnp.float32).astype(jnp.bfloat16)
    places = jnp.arange(STREAM_LENGTH, dtype=jnp.int32)
    live_mask = places < length
    key_rows = jnp.where(live_mask[:, None], key_rows, jnp.zeros_like(key_rows))
    value_rows = jnp.where(live_mask[:, None], value_rows, jnp.zeros_like(value_rows))
    decay_rates = jnp.where(live_mask[None, :], decay_log, jnp.zeros_like(decay_log))
    blocks = STREAM_LENGTH // SPAN
    query_blocks = queries.astype(jnp.float32).reshape(blocks, SPAN, RETENTION_HEADS, HEAD_DIM)
    key_blocks = key_rows.astype(jnp.float32).reshape(blocks, SPAN, RETENTION_HEADS, HEAD_DIM)
    value_blocks = value_rows.astype(jnp.float32).reshape(blocks, SPAN, RETENTION_HEADS, HEAD_DIM)
    within = jnp.cumsum(decay_rates.reshape(RETENTION_HEADS, blocks, SPAN), axis=-1).transpose(1, 0, 2)
    causal = jnp.arange(SPAN)[:, None] >= jnp.arange(SPAN)[None, :]

    def advance(carried, inputs):
        query_c, key_c, value_c, within_c = inputs
        scores = jnp.einsum('chd,ehd->hce', query_c, key_c, precision=HIGHEST_PRECISION)
        decay_gaps = jnp.where(causal, within_c[:, :, None] - within_c[:, None, :], 0.0)
        weights = rounded(jnp.where(causal, scores * jnp.exp(decay_gaps), 0.0))
        inner_part = jnp.einsum('hce,ehd->chd', weights, value_c, precision=HIGHEST_PRECISION)
        cross_part = jnp.einsum('chd,hde->che', query_c, carried, precision=HIGHEST_PRECISION)
        cross_part = cross_part * jnp.exp(within_c).T[:, :, None]
        block_ends = within_c[:, -1]
        decayed = rounded(key_c * jnp.exp(block_ends[None, :] - within_c.T)[:, :, None])
        growth = jnp.einsum('chd,che->hde', decayed, value_c, precision=HIGHEST_PRECISION)
        carried = jnp.exp(block_ends)[:, None, None] * carried + growth
        return (carried, inner_part + cross_part)
    closing, retained = lax.scan(advance, start_state, (query_blocks, key_blocks, value_blocks, within))
    retained = retained.reshape(STREAM_LENGTH, RETENTION_HEADS, HEAD_DIM)
    average = lax.optimization_barrier(jnp.mean(retained, axis=-1, keepdims=True))
    centered = retained - average
    spread = lax.optimization_barrier(jnp.mean(centered * centered, axis=-1, keepdims=True))
    normed = jnp.where(live_mask[:, None, None], centered * lax.rsqrt(spread + EPSILON), 0.0)
    normed = normed.reshape(STREAM_LENGTH, D).astype(jnp.bfloat16)
    features = jnp.dot(normed, whiten, preferred_element_type=jnp.float32).astype(jnp.bfloat16)
    return (features, closing)

def reference(tokens, w_query, w_key, w_value, decay_log, lengths, sources, targets, stash, whiten):
    initial = stash[sources]

    def per_asset(inputs):
        asset_tokens, asset_decay, asset_length, asset_start, asset_whiten = inputs
        return one_asset(asset_tokens, asset_decay, asset_length, asset_start, asset_whiten, w_query, w_key, w_value)
    features, closings = lax.map(per_asset, (tokens, decay_log, lengths, initial, whiten))
    kept_states = jnp.zeros_like(stash).at[targets].set(closings)
    return (features, kept_states)
```

```python
import functools
import jax
import jax.numpy as jnp
from jax import lax
from jax.experimental import pallas as pl
from jax.experimental.pallas import tpu as pltpu
from jax.sharding import PartitionSpec as P

HEADS = 8
DIM = 128
STEPS = 512
WIDTH = 1024
PAIR = 2 * DIM
HALF = 256
EPSILON = 1e-05
LOG2E = 1.4426950408889634
FAR = -1e30


def running_sum(rates):
    lane = lax.broadcasted_iota(jnp.int32, rates.shape, 1)
    shift = 1
    while shift < STEPS:
        moved = pltpu.roll(rates, shift, 1)
        rates = rates + jnp.where(lane >= shift, moved, 0.0)
        shift *= 2
    return rates


def keys_kernel(valid_ref, tokens_ref, w_key_ref, w_value_ref, decay_ref,
                total_ref, keys_ref, values_ref, sums_ref, live_tokens):
    pair = pl.program_id(0)
    valid = valid_ref[0] - lax.axis_index("seq") * STEPS

    @pl.when(pair == 0)
    def _():
        lane = lax.broadcasted_iota(jnp.int32, (HEADS, STEPS), 1)
        rates = jnp.where(lane < valid, decay_ref[...] * LOG2E, 0.0)
        sums = running_sum(rates)
        sums_ref[...] = sums
        growth = jnp.broadcast_to(sums[:, STEPS - 1:], (HEADS, DIM))
        total_ref[:, HEADS] = jnp.broadcast_to(growth[None], (16, HEADS, DIM))
        step = lax.broadcasted_iota(jnp.int32, (STEPS, DIM), 0)
        for g in range(WIDTH // DIM):
            part = tokens_ref[:, g * DIM:(g + 1) * DIM]
            live_tokens[:, g * DIM:(g + 1) * DIM] = jnp.where(
                step < valid, part.astype(jnp.float32), 0.0).astype(jnp.bfloat16)

    tokens = live_tokens[...]
    keys = jnp.dot(tokens, w_key_ref[...], preferred_element_type=jnp.float32)
    keys = (keys * DIM ** (-0.5)).astype(jnp.bfloat16)
    values = jnp.dot(tokens, w_value_ref[...], preferred_element_type=jnp.float32).astype(jnp.bfloat16)
    keys_t = keys.T
    keys_ref[...] = keys_t
    values_ref[...] = values
    for j in range(2):
        head = 2 * pair + j
        row = sums_ref[pl.ds(head, 1), :]
        tail = jnp.exp2(row[:, STEPS - 1:] - row)
        decayed = (keys_t[j * DIM:(j + 1) * DIM].astype(jnp.float32) * tail).astype(jnp.bfloat16)
        total = jnp.dot(decayed, values[:, j * DIM:(j + 1) * DIM], preferred_element_type=jnp.float32)
        total_ref[:, head] = total.reshape(16, 8, DIM)


def keys_call(valid, tokens, w_key, w_value, decay):
    return pl.pallas_call(
        keys_kernel,
        grid_spec=pltpu.PrefetchScalarGridSpec(
            num_scalar_prefetch=1,
            grid=(4,),
            in_specs=[
                pl.BlockSpec((STEPS, WIDTH), lambda i, s: (0, 0)),
                pl.BlockSpec((WIDTH, PAIR), lambda i, s: (0, i)),
                pl.BlockSpec((WIDTH, PAIR), lambda i, s: (0, i)),
                pl.BlockSpec((HEADS, STEPS), lambda i, s: (0, 0)),
            ],
            out_specs=[
                pl.BlockSpec((16, HEADS + 1, 8, DIM), lambda i, s: (0, 0, 0, 0)),
                pl.BlockSpec((PAIR, STEPS), lambda i, s: (i, 0)),
                pl.BlockSpec((STEPS, PAIR), lambda i, s: (0, i)),
                pl.BlockSpec((HEADS, STEPS), lambda i, s: (0, 0)),
            ],
            scratch_shapes=[pltpu.VMEM((STEPS, WIDTH), jnp.bfloat16)],
        ),
        out_shape=[
            jax.ShapeDtypeStruct((16, HEADS + 1, 8, DIM), jnp.float32),
            jax.ShapeDtypeStruct((WIDTH, STEPS), jnp.bfloat16),
            jax.ShapeDtypeStruct((STEPS, WIDTH), jnp.bfloat16),
            jax.ShapeDtypeStruct((HEADS, STEPS), jnp.float32),
        ],
        compiler_params=pltpu.CompilerParams(vmem_limit_bytes=40 * 1024 * 1024),
        cost_estimate=pl.CostEstimate(flops=2 * 2 * STEPS * WIDTH * WIDTH, bytes_accessed=8 * 2 ** 20, transcendentals=0),
        name="keys_values",
    )(valid, tokens, w_key, w_value, decay)


def inner_kernel(tokens_ref, w_query_ref, keys_ref, values_ref, sums_ref, queries_ref, inner_ref, columns):
    pair = pl.program_id(0)

    @pl.when(pair == 0)
    def _():
        columns[...] = jnp.concatenate([sums_ref[...], jnp.zeros((DIM - HEADS, STEPS), jnp.float32)], 0).T

    queries = jnp.dot(tokens_ref[...], w_query_ref[...], preferred_element_type=jnp.float32).astype(jnp.bfloat16)
    queries_ref[...] = queries
    turned = pltpu.roll(columns[...], (DIM - 2 * pair) % DIM, 1)
    causal = (lax.broadcasted_iota(jnp.int32, (DIM, DIM), 0)
              >= lax.broadcasted_iota(jnp.int32, (DIM, DIM), 1))
    for j in range(2):
        head = 2 * pair + j
        lanes = slice(j * DIM, (j + 1) * DIM)
        row = sums_ref[pl.ds(head, 1), :]
        column = jnp.broadcast_to(turned[:, j:j + 1], (STEPS, DIM))
        middle = row[:, HALF - 1:HALF]
        state = None
        for c in range(2):
            base = c * HALF
            k_t = keys_ref[lanes, base:base + HALF]
            v = values_ref[base:base + HALF, lanes]
            for s in range(2):
                rows = slice(base + s * DIM, base + (s + 1) * DIM)
                q = queries[rows, lanes]
                wide = (s + 1) * DIM
                scores = jnp.dot(q, k_t[:, :wide], preferred_element_type=jnp.float32)
                parts = []
                for b in range(s + 1):
                    gap = column[rows] - row[:, base + b * DIM:base + (b + 1) * DIM]
                    if b == s:
                        gap = jnp.where(causal, gap, FAR)
                    parts.append((scores[:, b * DIM:(b + 1) * DIM] * jnp.exp2(gap)).astype(jnp.bfloat16))
                weights = parts[0] if s == 0 else jnp.concatenate(parts, 1)
                part = jnp.dot(weights, v[:wide], preferred_element_type=jnp.float32)
                if c == 1:
                    cross = jnp.dot(jnp.concatenate([q, q], 1), state, preferred_element_type=jnp.float32)
                    part = part + cross * jnp.exp2(column[rows] - middle)
                inner_ref[rows, lanes] = part
            if c == 0:
                tail = jnp.exp2(middle - row[:, :HALF])
                decayed = (k_t.astype(jnp.float32) * tail).astype(jnp.bfloat16)
                state = split(jnp.dot(decayed, v, preferred_element_type=jnp.float32))


def split(state):
    high = state.astype(jnp.bfloat16)
    low = (state - high.astype(jnp.float32)).astype(jnp.bfloat16)
    return jnp.concatenate([high, low], 0)


def inner_call(tokens, w_query, keys, values, sums):
    return pl.pallas_call(
        inner_kernel,
        grid=(4,),
        in_specs=[
            pl.BlockSpec((STEPS, WIDTH), lambda i: (0, 0)),
            pl.BlockSpec((WIDTH, PAIR), lambda i: (0, i)),
            pl.BlockSpec((PAIR, STEPS), lambda i: (i, 0)),
            pl.BlockSpec((STEPS, PAIR), lambda i: (0, i)),
            pl.BlockSpec((HEADS, STEPS), lambda i: (0, 0)),
        ],
        out_specs=[
            pl.BlockSpec((STEPS, PAIR), lambda i: (0, i)),
            pl.BlockSpec((STEPS, PAIR), lambda i: (0, i)),
        ],
        out_shape=[
            jax.ShapeDtypeStruct((STEPS, WIDTH), jnp.bfloat16),
            jax.ShapeDtypeStruct((STEPS, WIDTH), jnp.float32),
        ],
        scratch_shapes=[pltpu.VMEM((STEPS, DIM), jnp.float32)],
        compiler_params=pltpu.CompilerParams(vmem_limit_bytes=40 * 1024 * 1024),
        cost_estimate=pl.CostEstimate(flops=2 * STEPS * WIDTH * WIDTH * 3 // 2, bytes_accessed=8 * 2 ** 20, transcendentals=0),
        name="queries_inner",
    )(tokens, w_query, keys, values, sums)


def scan_kernel(received_ref, start_ref, carried_ref, closing_ref):
    for head in range(HEADS):
        state = start_ref[head]
        for shard in range(16):
            carried_ref[shard, head] = state
            growth = jnp.exp2(received_ref[shard, HEADS, head:head + 1, :])
            state = growth * state + received_ref[shard, head]
        closing_ref[head] = state


def scan_call(received, start):
    return pl.pallas_call(
        scan_kernel,
        out_shape=[
            jax.ShapeDtypeStruct((16, HEADS, 8, DIM), jnp.float32),
            jax.ShapeDtypeStruct((HEADS, 8, DIM), jnp.float32),
        ],
        compiler_params=pltpu.CompilerParams(vmem_limit_bytes=40 * 1024 * 1024),
        cost_estimate=pl.CostEstimate(flops=2 ** 20, bytes_accessed=2 ** 20, transcendentals=0),
        name="scan_rows",
    )(received, start)


ROWS = 256


def outer_kernel(valid_ref, queries_ref, inner_ref, state_ref, sums_ref, whiten_ref, features_ref, normed, states, columns):
    strip = pl.program_id(0)
    valid = valid_ref[0] - lax.axis_index("seq") * STEPS

    @pl.when(strip == 0)
    def _():
        for head in range(HEADS):
            states[head] = split(state_ref[:, head].reshape(DIM, DIM))
        columns[...] = jnp.concatenate([sums_ref[...], jnp.zeros((DIM - HEADS, STEPS), jnp.float32)], 0).T

    base = pl.multiple_of(strip * ROWS, ROWS)
    column = columns[pl.ds(base, ROWS), :]
    column = jnp.exp2(column)
    step = base + lax.broadcasted_iota(jnp.int32, (ROWS, DIM), 0)
    alive = step < valid
    for head in range(HEADS):
        lanes = slice(head * DIM, (head + 1) * DIM)
        q = queries_ref[:, lanes]
        cross = jnp.dot(jnp.concatenate([q, q], 1), states[head], preferred_element_type=jnp.float32)
        retained = inner_ref[:, lanes] + cross * column[:, head:head + 1]
        average = jnp.mean(retained, axis=1, keepdims=True)
        centered = retained - average
        spread = jnp.mean(centered * centered, axis=1, keepdims=True)
        out = centered * lax.rsqrt(spread + EPSILON)
        normed[:, lanes] = jnp.where(alive, out, 0.0).astype(jnp.bfloat16)
    features_ref[...] = jnp.dot(normed[...], whiten_ref[...], preferred_element_type=jnp.float32).astype(jnp.bfloat16)


def outer_call(valid, queries, inner, state, sums, whiten):
    return pl.pallas_call(
        outer_kernel,
        grid_spec=pltpu.PrefetchScalarGridSpec(
            num_scalar_prefetch=1,
            grid=(STEPS // ROWS,),
            in_specs=[
                pl.BlockSpec((ROWS, WIDTH), lambda i, s: (i, 0)),
                pl.BlockSpec((ROWS, WIDTH), lambda i, s: (i, 0)),
                pl.BlockSpec((16, HEADS, 8, DIM), lambda i, s: (0, 0, 0, 0)),
                pl.BlockSpec((HEADS, STEPS), lambda i, s: (0, 0)),
                pl.BlockSpec((WIDTH, WIDTH), lambda i, s: (0, 0)),
            ],
            out_specs=pl.BlockSpec((ROWS, WIDTH), lambda i, s: (i, 0)),
            scratch_shapes=[
                pltpu.VMEM((ROWS, WIDTH), jnp.bfloat16),
                pltpu.VMEM((HEADS, PAIR, DIM), jnp.bfloat16),
                pltpu.VMEM((STEPS, DIM), jnp.float32),
            ],
        ),
        out_shape=jax.ShapeDtypeStruct((STEPS, WIDTH), jnp.bfloat16),
        compiler_params=pltpu.CompilerParams(vmem_limit_bytes=40 * 1024 * 1024),
        cost_estimate=pl.CostEstimate(flops=2 * STEPS * WIDTH * WIDTH * 3 // 2, bytes_accessed=8 * 2 ** 20, transcendentals=0),
        name="outer_whiten",
    )(valid, queries, inner, state, sums, whiten)


def select_kernel(count, choose, *refs):
    route_ref, items, out_ref = refs[0], refs[1:-1], refs[-1]
    for slot, number in enumerate(choose(route_ref)):
        for k, (ref, at) in enumerate(listed(items)):
            @pl.when(number == k)
            def _(ref=ref, at=at):
                out_ref[slot] = ref[at]


def listed(items):
    return [(ref, at) for ref in items for at in range(ref.shape[0])]


def select_call(name, choose, count, route, *items):
    return pl.pallas_call(
        functools.partial(select_kernel, count, choose),
        in_specs=[pl.BlockSpec(memory_space=pltpu.SMEM)] + [pl.BlockSpec(memory_space=pltpu.VMEM)] * len(items),
        out_specs=pl.BlockSpec(memory_space=pltpu.VMEM),
        out_shape=jax.ShapeDtypeStruct((count, HEADS, 8, DIM), jnp.float32),
        cost_estimate=pl.CostEstimate(flops=1024, bytes_accessed=2 ** 17, transcendentals=0),
        name=name,
    )(route, *items)


def giver(inverted, route_ref, slot):
    if not inverted:
        return route_ref[slot]
    found = jnp.int32(0)
    for k in range(1, 16):
        found = jnp.where(route_ref[k] == slot, k, found)
    return found


def third_hop(inverted, route_ref):
    me = lax.axis_index("asset")
    return [(giver(inverted, route_ref, me ^ 4 ^ (8 * t)) ^ me) & 3 for t in range(2)]


def fourth_hop(inverted, route_ref):
    me = lax.axis_index("asset")
    source = giver(inverted, route_ref, me ^ 8)
    return [jnp.where((source >> 2) == (me >> 2), (source ^ me) & 3, 5)]


def arrival(inverted, route_ref):
    me = lax.axis_index("asset")
    source = giver(inverted, route_ref, me)
    near = jnp.where((source >> 2) == (me >> 2), (source ^ me) & 3, 4)
    return [jnp.where((source >> 3) == (me >> 3), near, 6)]


def swap(value, bit):
    return lax.ppermute(value, "asset", [(k, k ^ bit) for k in range(16)])


def on_device(tokens, w_query, w_key, w_value, decay_log, lengths, sources, targets, stash, whiten):
    tokens, decay, whiten = tokens[0], decay_log[0], whiten[0]
    own = stash
    one = swap(own, 1)
    pair = jnp.concatenate([own, one], 0)
    total, keys, values, sums = keys_call(lengths, tokens, w_key, w_value, decay)
    two = swap(pair, 2)
    third = select_call("hop_three", functools.partial(third_hop, False), 2, sources, own, one, two)
    four = swap(third, 4)
    fourth = select_call("hop_four", functools.partial(fourth_hop, False), 1, sources, own, one, two, four)
    eight = swap(fourth, 8)
    received = lax.all_to_all(total, "seq", 0, 0, tiled=True)
    queries, inner = inner_call(tokens, w_query, keys, values, sums)
    start = select_call("arrived", functools.partial(arrival, False), 1, sources, own, one, two, four, eight)
    carried, closing = scan_call(received, start[0])
    own = closing[None]
    one = swap(own, 1)
    pair = jnp.concatenate([own, one], 0)
    two = swap(pair, 2)
    state = lax.all_to_all(carried, "seq", 0, 0, tiled=True)
    third = select_call("hop_three", functools.partial(third_hop, True), 2, targets, own, one, two)
    four = swap(third, 4)
    fourth = select_call("hop_four", functools.partial(fourth_hop, True), 1, targets, own, one, two, four)
    eight = swap(fourth, 8)
    features = outer_call(lengths, queries, inner, state, sums, whiten)
    kept = select_call("arrived", functools.partial(arrival, True), 1, targets, own, one, two, four, eight)
    return (features[None], kept)


def solution(mesh):
    return jax.shard_map(
        on_device,
        mesh=mesh,
        in_specs=(
            P("asset", "seq", None),
            P(),
            P(),
            P(),
            P("asset", None, "seq"),
            P("asset"),
            P(),
            P(),
            P("asset", None, "seq", None),
            P("asset", None, None),
        ),
        out_specs=(P("asset", "seq", None), P("asset", None, "seq", None)),
        check_vma=False,
    )
```

```python
import functools
import jax
import jax.numpy as jnp
from jax import lax
from jax.experimental import pallas as pl
from jax.experimental.pallas import tpu as pltpu
from jax.sharding import PartitionSpec as P

HEADS = 8
DIM = 128
STEPS = 512
WIDTH = 1024
PAIR = 2 * DIM
HALF = 256
SHARDS = 16
EPSILON = 1e-05
LOG2E = 1.4426950408889634
FAR = -1e30
MIB = 1024 * 1024
IN_HBM = pl.BlockSpec(memory_space=pltpu.HBM)
IN_VMEM = pl.BlockSpec(memory_space=pltpu.VMEM)
IN_SMEM = pl.BlockSpec(memory_space=pltpu.SMEM)
DMA = pltpu.SemaphoreType.DMA


def lanes_of(number, size=PAIR):
    return slice(number * size, (number + 1) * size)


def params(mib):
    return pltpu.CompilerParams(vmem_limit_bytes=mib * MIB)


def work(flops, nbytes):
    return pl.CostEstimate(flops=flops, bytes_accessed=nbytes, transcendentals=0)


def running_sum(rates):
    lane = lax.broadcasted_iota(jnp.int32, rates.shape, 1)
    shift = 1
    while shift < STEPS:
        moved = pltpu.roll(rates, shift, 1)
        rates = rates + jnp.where(lane >= shift, moved, 0.0)
        shift *= 2
    return rates


def split(state):
    high = state.astype(jnp.bfloat16)
    low = (state - high.astype(jnp.float32)).astype(jnp.bfloat16)
    return jnp.concatenate([high, low], 0)


def turned(sums):
    padding = jnp.zeros((DIM - HEADS, STEPS), jnp.float32)
    return jnp.concatenate([sums, padding], 0).T


def local_kernel(lengths_ref, tokens_hbm, w_query_hbm, w_key_hbm, w_value_hbm, decay_hbm,
                 total_hbm, mixed_hbm,
                 tokens_ref, w_query_ref, w_key_ref, w_value_ref, decay_ref,
                 keys_ref, values_ref, total_ref, mixed_ref, in_sems, out_sems):
    copies = []
    for at, (source, target) in enumerate((
            (decay_hbm, decay_ref), (tokens_hbm, tokens_ref), (w_key_hbm, w_key_ref),
            (w_value_hbm, w_value_ref), (w_query_hbm, w_query_ref))):
        copies.append(pltpu.make_async_copy(source, target, in_sems.at[at]))
        copies[at].start()
    outs = []

    def send(source, target):
        outs.append(pltpu.make_async_copy(source, target, out_sems.at[len(outs)]))
        outs[-1].start()

    valid = lengths_ref[0] - lax.axis_index("seq") * STEPS
    copies[0].wait()
    lane = lax.broadcasted_iota(jnp.int32, (HEADS, STEPS), 1)
    sums = running_sum(jnp.where(lane < valid, decay_ref[...] * LOG2E, 0.0))
    growth = jnp.broadcast_to(sums[:, STEPS - 1:], (HEADS, DIM))
    total_ref[:, HEADS] = jnp.broadcast_to(growth[None], (SHARDS, HEADS, DIM))
    tails = jnp.exp2(sums[:, STEPS - 1:] - sums)
    columns = turned(sums)
    alive = lax.broadcasted_iota(jnp.int32, (STEPS, PAIR), 0) < valid
    causal = (lax.broadcasted_iota(jnp.int32, (DIM, DIM), 0)
              >= lax.broadcasted_iota(jnp.int32, (DIM, DIM), 1))
    for copy in copies[1:4]:
        copy.wait()
    tokens = tokens_ref[...]
    for pair in range(4):
        lanes = lanes_of(pair)
        keys = jnp.dot(tokens, w_key_ref[:, lanes], preferred_element_type=jnp.float32)
        keys_t = jnp.where(alive, keys * DIM ** (-0.5), 0.0).astype(jnp.bfloat16).T
        values = jnp.dot(tokens, w_value_ref[:, lanes], preferred_element_type=jnp.float32)
        values = jnp.where(alive, values, 0.0).astype(jnp.bfloat16)
        keys_ref[lanes, :] = keys_t
        values_ref[:, lanes] = values
        for j in range(2):
            head = 2 * pair + j
            own = lanes_of(j, DIM)
            decayed = (keys_t[own].astype(jnp.float32) * tails[head:head + 1]).astype(jnp.bfloat16)
            total = jnp.dot(decayed, values[:, own], preferred_element_type=jnp.float32)
            total_ref[:, head] = total.reshape(SHARDS, 8, DIM)
    send(total_ref, total_hbm)
    copies[4].wait()
    for pair in range(4):
        lanes = lanes_of(pair)
        queries = jnp.dot(tokens, w_query_ref[:, lanes], preferred_element_type=jnp.float32).astype(jnp.bfloat16)
        for j in range(2):
            head = 2 * pair + j
            own = lanes_of(head, DIM)
            attend(causal, sums[head:head + 1], columns[:, head:head + 1], queries[:, lanes_of(j, DIM)],
                   keys_ref[own, :], values_ref[:, own], own, mixed_ref)
        if pair % 2 == 1:
            done = slice((pair - 1) * PAIR, (pair + 1) * PAIR)
            send(mixed_ref.at[:, :, done], mixed_hbm.at[:, :, done])
    for copy in outs:
        copy.wait()


def attend(causal, row, column, queries, keys_t, values, own, mixed_ref):
    first = slice(0, HALF)
    middle = row[:, HALF - 1:HALF]
    decayed = (keys_t[:, first].astype(jnp.float32) * jnp.exp2(middle - row[:, first])).astype(jnp.bfloat16)
    state = split(jnp.dot(decayed, values[first], preferred_element_type=jnp.float32))
    column = jnp.broadcast_to(column, (STEPS, DIM))
    mixed_ref[0, :, own] = (queries.astype(jnp.float32) * jnp.exp2(column)).astype(jnp.bfloat16)
    for c in range(2):
        rows = lanes_of(c)
        q = queries[rows]
        scores = jnp.dot(q, keys_t[:, rows], preferred_element_type=jnp.float32)
        strips = []
        for s in range(2):
            here = column[c * HALF + s * DIM:c * HALF + (s + 1) * DIM]
            parts = []
            for b in range(s + 1):
                gap = here - row[:, c * HALF + b * DIM:c * HALF + (b + 1) * DIM]
                if b == s:
                    gap = jnp.where(causal, gap, FAR)
                score = scores[s * DIM:(s + 1) * DIM, b * DIM:(b + 1) * DIM]
                parts.append((score * jnp.exp2(gap)).astype(jnp.bfloat16))
            if s == 0:
                parts.append(jnp.zeros((DIM, DIM), jnp.bfloat16))
            strips.append(jnp.concatenate(parts, 1))
        weights = jnp.concatenate(strips, 0)
        part = jnp.dot(weights, values[rows], preferred_element_type=jnp.float32)
        if c == 1:
            cross = jnp.dot(jnp.concatenate([q, q], 1), state, preferred_element_type=jnp.float32)
            part = part + cross * jnp.exp2(column[HALF:] - middle)
        part = part - jnp.mean(part, axis=1, keepdims=True)
        mixed_ref[1, rows, own] = part.astype(jnp.bfloat16)


def local_call(lengths, tokens, w_query, w_key, w_value, decay):
    return pl.pallas_call(
        local_kernel,
        in_specs=[IN_SMEM] + [IN_HBM] * 5,
        out_specs=[IN_HBM] * 2,
        out_shape=[
            jax.ShapeDtypeStruct((SHARDS, HEADS + 1, 8, DIM), jnp.float32),
            jax.ShapeDtypeStruct((2, STEPS, WIDTH), jnp.bfloat16),
        ],
        scratch_shapes=[
            pltpu.VMEM((STEPS, WIDTH), jnp.bfloat16),
            pltpu.VMEM((WIDTH, WIDTH), jnp.bfloat16),
            pltpu.VMEM((WIDTH, WIDTH), jnp.bfloat16),
            pltpu.VMEM((WIDTH, WIDTH), jnp.bfloat16),
            pltpu.VMEM((HEADS, STEPS), jnp.float32),
            pltpu.VMEM((WIDTH, STEPS), jnp.bfloat16),
            pltpu.VMEM((STEPS, WIDTH), jnp.bfloat16),
            pltpu.VMEM((SHARDS, HEADS + 1, 8, DIM), jnp.float32),
            pltpu.VMEM((2, STEPS, WIDTH), jnp.bfloat16),
            DMA((5,)),
            DMA((3,)),
        ],
        compiler_params=params(62),
        cost_estimate=work(2 * STEPS * WIDTH * WIDTH * 4, 10 * MIB),
        name="local_pass",
    )(lengths, tokens, w_query, w_key, w_value, decay)


def scan_kernel(sources_ref, received_ref, *refs):
    items = refs[:7]
    carried_hbm, closing_ref, start_ref, rows_ref, sems = refs[7:]
    number = landing(sources_ref[lax.axis_index("asset")])
    for k, item in enumerate(items):
        @pl.when(number == k)
        def _(item=item):
            start_ref[...] = item[...]
    states = [start_ref[head] for head in range(HEADS)]
    outs = []
    for shard in range(SHARDS):
        for head in range(HEADS):
            rows_ref[shard, head] = states[head]
            growth = jnp.exp2(received_ref[shard, HEADS, head:head + 1, :])
            states[head] = growth * states[head] + received_ref[shard, head]
        if shard % 4 == 3:
            done = slice(shard - 3, shard + 1)
            outs.append(pltpu.make_async_copy(rows_ref.at[done], carried_hbm.at[done], sems.at[shard // 4]))
            outs[-1].start()
    for head in range(HEADS):
        closing_ref[head] = states[head]
    for copy in outs:
        copy.wait()


def scan_call(sources, received, items):
    return pl.pallas_call(
        scan_kernel,
        in_specs=[IN_SMEM] + [IN_VMEM] * 8,
        out_specs=[IN_HBM, IN_VMEM],
        out_shape=[
            jax.ShapeDtypeStruct((SHARDS, HEADS, 8, DIM), jnp.float32),
            jax.ShapeDtypeStruct((HEADS, 8, DIM), jnp.float32),
        ],
        scratch_shapes=[
            pltpu.VMEM((HEADS, 8, DIM), jnp.float32),
            pltpu.VMEM((SHARDS, HEADS, 8, DIM), jnp.float32),
            DMA((4,)),
        ],
        compiler_params=params(8),
        cost_estimate=work(MIB, 2 * MIB),
        name="scan_rows",
    )(sources, received, *items)


STRIP = 512


def outer_kernel(lengths_ref, mixed_ref, state_ref, whiten_ref,
                 features_hbm, out_ref, out_sems):
    valid = lengths_ref[0] - lax.axis_index("seq") * STEPS
    states = []
    for head in range(HEADS):
        state = state_ref[:, head].reshape(DIM, DIM)
        states.append(split(state - jnp.mean(state, axis=1, keepdims=True)))
    same = (lax.broadcasted_iota(jnp.int32, (PAIR, PAIR), 0) // DIM
            == lax.broadcasted_iota(jnp.int32, (PAIR, PAIR), 1) // DIM)
    averaging = jnp.where(same, 1.0 / DIM, 0.0).astype(jnp.bfloat16)
    out_copies = []
    for strip in range(STEPS // STRIP):
        rows = lanes_of(strip, STRIP)
        alive = strip * STRIP + lax.broadcasted_iota(jnp.int32, (STRIP, PAIR), 0) < valid
        parts = []
        for pair in range(4):
            halves = []
            for head in (2 * pair, 2 * pair + 1):
                own = lanes_of(head, DIM)
                q = mixed_ref[0, rows, own]
                cross = jnp.dot(jnp.concatenate([q, q], 1), states[head], preferred_element_type=jnp.float32)
                halves.append(mixed_ref[1, rows, own].astype(jnp.float32) + cross)
            centered = jnp.concatenate(halves, 1)
            squares = (centered * centered).astype(jnp.bfloat16)
            spread = jnp.dot(squares, averaging, preferred_element_type=jnp.float32)
            scale = jnp.where(alive, lax.rsqrt(spread + EPSILON), 0.0)
            parts.append((centered * scale).astype(jnp.bfloat16))
        out_ref[rows, :] = jnp.dot(
            jnp.concatenate(parts, 1), whiten_ref[...], preferred_element_type=jnp.float32).astype(jnp.bfloat16)
        out_copies.append(pltpu.make_async_copy(
            out_ref.at[rows, :], features_hbm.at[rows, :], out_sems.at[strip]))
        out_copies[strip].start()
    for copy in out_copies:
        copy.wait()


def outer_call(lengths, mixed, state, whiten):
    return pl.pallas_call(
        outer_kernel,
        in_specs=[IN_SMEM] + [IN_VMEM] * 3,
        out_specs=IN_HBM,
        out_shape=jax.ShapeDtypeStruct((STEPS, WIDTH), jnp.bfloat16),
        scratch_shapes=[
            pltpu.VMEM((STEPS, WIDTH), jnp.bfloat16),
            DMA((STEPS // STRIP,)),
        ],
        compiler_params=params(16),
        cost_estimate=work(2 * STEPS * WIDTH * WIDTH * 3 // 2, 4 * MIB),
        name="outer_whiten",
    )(lengths, mixed, state, whiten)


def origin(targets_ref, slot):
    asset = jnp.int32(0)
    for k in range(1, SHARDS):
        asset = jnp.where(targets_ref[k] == slot, k, asset)
    return asset


def landing(source):
    me = lax.axis_index("asset")
    steps = (me ^ source) & 3
    return jnp.where(steps == 0, (me ^ source) >> 2, 3 + steps)


def near_kernel(inverted, route_ref, *refs):
    items, outs = refs[:4], refs[5:8]
    me = lax.axis_index("asset")
    for j, out in enumerate(outs, 1):
        slot = me ^ j
        source = origin(route_ref, slot) if inverted else route_ref[slot]
        number = ((me ^ source) >> 2) & 3
        for k, item in enumerate(items):
            @pl.when(number == k)
            def _(item=item, out=out):
                out[...] = item[...]


def near_call(inverted, route, items, passed):
    return pl.pallas_call(
        functools.partial(near_kernel, inverted),
        in_specs=[IN_SMEM] + [IN_VMEM] * 4 + [pl.BlockSpec(memory_space=pl.ANY)],
        out_specs=[IN_VMEM] * 3 + [pl.BlockSpec(memory_space=pl.ANY)],
        out_shape=[jax.ShapeDtypeStruct((HEADS, 8, DIM), jnp.float32)] * 3
        + [jax.ShapeDtypeStruct(passed.shape, passed.dtype)],
        input_output_aliases={5: 3},
        compiler_params=params(63),
        cost_estimate=work(1024, 2 ** 17),
        name="near_rows",
    )(route, *items, passed)


def kept_kernel(targets_ref, *refs):
    items, kept_hbm, sem = refs[:7], refs[7], refs[8]
    number = landing(origin(targets_ref, lax.axis_index("asset")))
    for k, item in enumerate(items):
        @pl.when(number == k)
        def _(item=item):
            copy = pltpu.make_async_copy(item, kept_hbm.at[0], sem)
            copy.start()
            copy.wait()


def kept_call(targets, items):
    return pl.pallas_call(
        kept_kernel,
        in_specs=[IN_SMEM] + [pl.BlockSpec(memory_space=pl.ANY)] * 7,
        out_specs=pl.BlockSpec(memory_space=pl.ANY),
        out_shape=jax.ShapeDtypeStruct((1, HEADS, 8, DIM), jnp.float32),
        scratch_shapes=[DMA],
        compiler_params=params(8),
        cost_estimate=work(1024, 2 ** 17),
        name="kept_rows",
    )(targets, *items)


def swap(value, bits):
    return lax.ppermute(value, "asset", [(k, k ^ bits) for k in range(SHARDS)])


def on_device(tokens, w_query, w_key, w_value, decay_log, lengths, sources, targets, stash, whiten):
    tokens, decay, whiten = tokens[0], decay_log[0], whiten[0]
    own = stash[0]
    items = [own] + [swap(own, 4 * k) for k in (1, 2, 3)]
    total, mixed = local_call(lengths, tokens, w_query, w_key, w_value, decay)
    *near, total = near_call(False, sources, items, total)
    items += [swap(item, k) for k, item in enumerate(near, 1)]
    received = lax.all_to_all(total, "seq", 0, 0, tiled=True)
    carried, closing = scan_call(sources, received, items)
    state = lax.all_to_all(carried, "seq", 0, 0, tiled=True)
    items = [closing] + [swap(closing, 4 * k) for k in (1, 2, 3)]
    features = outer_call(lengths, mixed, state, whiten)
    *near, features = near_call(True, targets, items, features)
    items += [swap(item, k) for k, item in enumerate(near, 1)]
    return (features[None], kept_call(targets, items))


def solution(mesh):
    return jax.shard_map(
        on_device,
        mesh=mesh,
        in_specs=(
            P("asset", "seq", None),
            P(),
            P(),
            P(),
            P("asset", None, "seq"),
            P("asset"),
            P(),
            P(),
            P("asset", None, "seq", None),
            P("asset", None, None),
        ),
        out_specs=(P("asset", "seq", None), P("asset", None, "seq", None)),
        check_vma=False,
    )
```

```python
import functools
import jax
import jax.numpy as jnp
from jax import lax
from jax.experimental import pallas as pl
from jax.experimental.pallas import tpu as pltpu
from jax.sharding import PartitionSpec as P

HEADS = 8
DIM = 128
STEPS = 512
WIDTH = 1024
PAIR = 2 * DIM
HALF = 256
SHARDS = 16
EPSILON = 1e-05
LOG2E = 1.4426950408889634
FAR = -1e30
MIB = 1024 * 1024
IN_HBM = pl.BlockSpec(memory_space=pltpu.HBM)
IN_VMEM = pl.BlockSpec(memory_space=pltpu.VMEM)
IN_SMEM = pl.BlockSpec(memory_space=pltpu.SMEM)
DMA = pltpu.SemaphoreType.DMA


def lanes_of(number, size=PAIR):
    return slice(number * size, (number + 1) * size)


def params(mib):
    return pltpu.CompilerParams(vmem_limit_bytes=mib * MIB)


def work(flops, nbytes):
    return pl.CostEstimate(flops=flops, bytes_accessed=nbytes, transcendentals=0)


def running_sum(rates):
    lane = lax.broadcasted_iota(jnp.int32, rates.shape, 1)
    shift = 1
    while shift < STEPS:
        moved = pltpu.roll(rates, shift, 1)
        rates = rates + jnp.where(lane >= shift, moved, 0.0)
        shift *= 2
    return rates


def split(state):
    high = state.astype(jnp.bfloat16)
    low = (state - high.astype(jnp.float32)).astype(jnp.bfloat16)
    return jnp.concatenate([high, low], 0)


def turned(sums):
    padding = jnp.zeros((DIM - HEADS, STEPS), jnp.float32)
    return jnp.concatenate([sums, padding], 0).T


def place():
    rank = lax.axis_index("seq")
    return rank & 3, rank >> 2


def fetch_kernel(stash_ref, own_ref):
    own_ref[...] = stash_ref[0]


def fetch_call(stash):
    return pl.pallas_call(
        fetch_kernel,
        in_specs=[IN_VMEM],
        out_specs=IN_VMEM,
        out_shape=jax.ShapeDtypeStruct((HEADS, 8, DIM), jnp.float32),
        compiler_params=params(8),
        cost_estimate=pl.CostEstimate(flops=2 ** 36, bytes_accessed=2 ** 30, transcendentals=2 ** 30),
        name="own_rows",
    )(stash)


def keys_kernel(lengths_ref, tokens_ref, w_key_ref, w_value_ref, decay_ref, *refs):
    quarters = refs[:4]
    keys_ref, values_ref, sums_ref, quarter_ref = refs[4:]
    valid = lengths_ref[0] - lax.axis_index("seq") * STEPS
    lane = lax.broadcasted_iota(jnp.int32, (HEADS, STEPS), 1)
    sums = running_sum(jnp.where(lane < valid, decay_ref[...] * LOG2E, 0.0))
    sums_ref[...] = sums
    growth = jnp.broadcast_to(sums[:, STEPS - 1:], (HEADS, DIM))
    tails = jnp.exp2(sums[:, STEPS - 1:] - sums)
    alive = lax.broadcasted_iota(jnp.int32, (STEPS, PAIR), 0) < valid
    tokens = tokens_ref[...]
    for pair in range(4):
        lanes = lanes_of(pair)
        keys = jnp.dot(tokens, w_key_ref[:, lanes], preferred_element_type=jnp.float32)
        keys_t = jnp.where(alive, keys * DIM ** (-0.5), 0.0).astype(jnp.bfloat16).T
        values = jnp.dot(tokens, w_value_ref[:, lanes], preferred_element_type=jnp.float32)
        values = jnp.where(alive, values, 0.0).astype(jnp.bfloat16)
        keys_ref[lanes, :] = keys_t
        values_ref[:, lanes] = values
        for j in range(2):
            head = 2 * pair + j
            own = lanes_of(j, DIM)
            decayed = (keys_t[own].astype(jnp.float32) * tails[head:head + 1]).astype(jnp.bfloat16)
            total = jnp.dot(decayed, values[:, own], preferred_element_type=jnp.float32)
            for block in range(SHARDS):
                quarter_ref[block % 4, (block // 4) * HEADS + head] = total[block * 8:(block + 1) * 8]
    x, _ = place()
    for k, out in enumerate(quarters):
        out[:32] = quarter_ref[x ^ k]
        out[32] = growth


def keys_call(lengths, tokens, w_key, w_value, decay):
    return pl.pallas_call(
        keys_kernel,
        in_specs=[IN_SMEM] + [IN_VMEM] * 4,
        out_specs=[IN_VMEM] * 7,
        out_shape=[jax.ShapeDtypeStruct((33, 8, DIM), jnp.float32)] * 4 + [
            jax.ShapeDtypeStruct((WIDTH, STEPS), jnp.bfloat16),
            jax.ShapeDtypeStruct((STEPS, WIDTH), jnp.bfloat16),
            jax.ShapeDtypeStruct((HEADS, STEPS), jnp.float32),
        ],
        scratch_shapes=[pltpu.VMEM((4, 32, 8, DIM), jnp.float32)],
        compiler_params=params(16),
        cost_estimate=work(2 * STEPS * WIDTH * WIDTH * 3, 16 * MIB),
        name="keys_values",
    )(lengths, tokens, w_key, w_value, decay)


def inner_kernel(tokens_ref, w_query_ref, keys_ref, values_ref, sums_ref, after_ref, mixed_ref):
    sums = sums_ref[...]
    columns = turned(sums)
    causal = (lax.broadcasted_iota(jnp.int32, (DIM, DIM), 0)
              >= lax.broadcasted_iota(jnp.int32, (DIM, DIM), 1))
    tokens = tokens_ref[...]
    for pair in range(4):
        lanes = lanes_of(pair)
        queries = jnp.dot(tokens, w_query_ref[:, lanes], preferred_element_type=jnp.float32).astype(jnp.bfloat16)
        for j in range(2):
            head = 2 * pair + j
            own = lanes_of(head, DIM)
            attend(causal, sums[head:head + 1], columns[:, head:head + 1], queries[:, lanes_of(j, DIM)],
                   keys_ref[own, :], values_ref[:, own], own, mixed_ref)


def inner_call(tokens, w_query, keys, values, sums, after):
    return pl.pallas_call(
        inner_kernel,
        in_specs=[IN_VMEM] * 5 + [pl.BlockSpec(memory_space=pl.ANY)],
        out_specs=IN_VMEM,
        out_shape=jax.ShapeDtypeStruct((2, STEPS, WIDTH), jnp.bfloat16),
        compiler_params=params(16),
        cost_estimate=work(2 * STEPS * WIDTH * WIDTH * 3, 5 * MIB),
        name="queries_inner",
    )(tokens, w_query, keys, values, sums, after)


def attend(causal, row, column, queries, keys_t, values, own, mixed_ref):
    first = slice(0, HALF)
    middle = row[:, HALF - 1:HALF]
    decayed = (keys_t[:, first].astype(jnp.float32) * jnp.exp2(middle - row[:, first])).astype(jnp.bfloat16)
    state = split(jnp.dot(decayed, values[first], preferred_element_type=jnp.float32))
    column = jnp.broadcast_to(column, (STEPS, DIM))
    mixed_ref[0, :, own] = (queries.astype(jnp.float32) * jnp.exp2(column)).astype(jnp.bfloat16)
    for c in range(2):
        rows = lanes_of(c)
        q = queries[rows]
        scores = jnp.dot(q, keys_t[:, rows], preferred_element_type=jnp.float32)
        strips = []
        for s in range(2):
            here = column[c * HALF + s * DIM:c * HALF + (s + 1) * DIM]
            parts = []
            for b in range(s + 1):
                gap = here - row[:, c * HALF + b * DIM:c * HALF + (b + 1) * DIM]
                if b == s:
                    gap = jnp.where(causal, gap, FAR)
                score = scores[s * DIM:(s + 1) * DIM, b * DIM:(b + 1) * DIM]
                parts.append((score * jnp.exp2(gap)).astype(jnp.bfloat16))
            if s == 0:
                parts.append(jnp.zeros((DIM, DIM), jnp.bfloat16))
            strips.append(jnp.concatenate(parts, 1))
        weights = jnp.concatenate(strips, 0)
        part = jnp.dot(weights, values[rows], preferred_element_type=jnp.float32)
        if c == 1:
            cross = jnp.dot(jnp.concatenate([q, q], 1), state, preferred_element_type=jnp.float32)
            part = part + cross * jnp.exp2(column[HALF:] - middle)
        part = part - jnp.mean(part, axis=1, keepdims=True)
        mixed_ref[1, rows, own] = part.astype(jnp.bfloat16)


def row_kernel(sources_ref, *refs):
    quarters, items = refs[:4], refs[4:11]
    ordered_ref, payload_ref = refs[11:]
    x, _ = place()
    number = landing(sources_ref[lax.axis_index("asset")])
    for k, item in enumerate(items):
        @pl.when(number == k)
        def _(item=item):
            payload_ref[33:41] = item[...]
    for k, quarter in enumerate(quarters):
        ordered_ref[x ^ k] = quarter[...]
    for row in range(32):
        head = row % HEADS
        state = ordered_ref[0, row]
        for shard in range(1, 4):
            state = jnp.exp2(ordered_ref[shard, 32, head:head + 1]) * state + ordered_ref[shard, row]
        payload_ref[row] = state
    growth = ordered_ref[0, 32]
    for shard in range(1, 4):
        growth = growth + ordered_ref[shard, 32]
    payload_ref[32] = growth


def row_call(sources, quarters, items):
    return pl.pallas_call(
        row_kernel,
        in_specs=[IN_SMEM] + [IN_VMEM] * 11,
        out_specs=[IN_VMEM] * 2,
        out_shape=[
            jax.ShapeDtypeStruct((4, 33, 8, DIM), jnp.float32),
            jax.ShapeDtypeStruct((41, 8, DIM), jnp.float32),
        ],
        compiler_params=params(8),
        cost_estimate=work(MIB, 16 * MIB),
        name="row_totals",
    )(sources, *quarters, *items)


def carry_kernel(*refs):
    payloads, ordered_ref, carried = refs[:4], refs[4], refs[6:10]
    closing_ref, rows_ref, carry_ref, final_ref = refs[10:]
    x, y = place()
    for m, payload in enumerate(payloads):
        rows_ref[y ^ m] = payload[...]
    for row in range(32):
        head, block = row % HEADS, row // HEADS
        state = rows_ref[block, 33 + head]
        carry = state
        for line in range(4):
            carry = jnp.where(y == line, state, carry)
            state = jnp.exp2(rows_ref[line, 32, head:head + 1]) * state + rows_ref[line, row]
        final_ref[block, head] = state
        carry_ref[0, row] = carry
        for shard in range(3):
            carry = jnp.exp2(ordered_ref[shard, 32, head:head + 1]) * carry + ordered_ref[shard, row]
            carry_ref[shard + 1, row] = carry
    for k, out in enumerate(carried):
        out[...] = carry_ref[x ^ k]
    closing_ref[...] = final_ref[y]


def carry_call(payloads, ordered, after):
    return pl.pallas_call(
        carry_kernel,
        in_specs=[IN_VMEM] * 5 + [pl.BlockSpec(memory_space=pl.ANY)],
        out_specs=[IN_VMEM] * 5,
        out_shape=[jax.ShapeDtypeStruct((32, 8, DIM), jnp.float32)] * 4
        + [jax.ShapeDtypeStruct((HEADS, 8, DIM), jnp.float32)],
        scratch_shapes=[
            pltpu.VMEM((4, 41, 8, DIM), jnp.float32),
            pltpu.VMEM((4, 32, 8, DIM), jnp.float32),
            pltpu.VMEM((4, HEADS, 8, DIM), jnp.float32),
        ],
        compiler_params=params(8),
        cost_estimate=work(MIB, 2 * MIB),
        name="carry_rows",
    )(*payloads, ordered, after)


STRIP = 512


def outer_kernel(lengths_ref, mixed_ref, *refs):
    quarters, whiten_ref, features_hbm, mark_ref, out_ref, state_ref, out_sems = refs[:4], *refs[4:]
    mark_ref[...] = jnp.zeros((8, DIM), jnp.float32)
    x, _ = place()
    for k, quarter in enumerate(quarters):
        for block in range(4):
            state_ref[4 * block + (x ^ k)] = quarter[block * HEADS:(block + 1) * HEADS]
    valid = lengths_ref[0] - lax.axis_index("seq") * STEPS
    states = []
    for head in range(HEADS):
        state = state_ref[:, head].reshape(DIM, DIM)
        states.append(split(state - jnp.mean(state, axis=1, keepdims=True)))
    same = (lax.broadcasted_iota(jnp.int32, (PAIR, PAIR), 0) // DIM
            == lax.broadcasted_iota(jnp.int32, (PAIR, PAIR), 1) // DIM)
    averaging = jnp.where(same, 1.0 / DIM, 0.0).astype(jnp.bfloat16)
    out_copies = []
    for strip in range(STEPS // STRIP):
        rows = lanes_of(strip, STRIP)
        alive = strip * STRIP + lax.broadcasted_iota(jnp.int32, (STRIP, PAIR), 0) < valid
        parts = []
        for pair in range(4):
            halves = []
            for head in (2 * pair, 2 * pair + 1):
                own = lanes_of(head, DIM)
                q = mixed_ref[0, rows, own]
                cross = jnp.dot(jnp.concatenate([q, q], 1), states[head], preferred_element_type=jnp.float32)
                halves.append(mixed_ref[1, rows, own].astype(jnp.float32) + cross)
            centered = jnp.concatenate(halves, 1)
            squares = (centered * centered).astype(jnp.bfloat16)
            spread = jnp.dot(squares, averaging, preferred_element_type=jnp.float32)
            scale = jnp.where(alive, lax.rsqrt(spread + EPSILON), 0.0)
            parts.append((centered * scale).astype(jnp.bfloat16))
        out_ref[rows, :] = jnp.dot(
            jnp.concatenate(parts, 1), whiten_ref[...], preferred_element_type=jnp.float32).astype(jnp.bfloat16)
        out_copies.append(pltpu.make_async_copy(
            out_ref.at[rows, :], features_hbm.at[rows, :], out_sems.at[strip]))
        out_copies[strip].start()
    for copy in out_copies:
        copy.wait()


def outer_call(lengths, mixed, quarters, whiten):
    return pl.pallas_call(
        outer_kernel,
        in_specs=[IN_SMEM] + [IN_VMEM] * 6,
        out_specs=[IN_HBM, IN_VMEM],
        out_shape=[
            jax.ShapeDtypeStruct((STEPS, WIDTH), jnp.bfloat16),
            jax.ShapeDtypeStruct((8, DIM), jnp.float32),
        ],
        scratch_shapes=[
            pltpu.VMEM((STEPS, WIDTH), jnp.bfloat16),
            pltpu.VMEM((SHARDS, HEADS, 8, DIM), jnp.float32),
            DMA((STEPS // STRIP,)),
        ],
        compiler_params=params(16),
        cost_estimate=work(2 * STEPS * WIDTH * WIDTH * 3 // 2, 4 * MIB),
        name="outer_whiten",
    )(lengths, mixed, *quarters, whiten)


def origin(targets_ref, slot):
    asset = jnp.int32(0)
    for k in range(1, SHARDS):
        asset = jnp.where(targets_ref[k] == slot, k, asset)
    return asset


def landing(source):
    me = lax.axis_index("asset")
    steps = (me ^ source) & 3
    return jnp.where(steps == 0, (me ^ source) >> 2, 3 + steps)


def near_kernel(inverted, route_ref, *refs):
    items, outs = refs[:4], refs[-3:]
    me = lax.axis_index("asset")
    for j, out in enumerate(outs, 1):
        slot = me ^ j
        source = origin(route_ref, slot) if inverted else route_ref[slot]
        number = ((me ^ source) >> 2) & 3
        for k, item in enumerate(items):
            @pl.when(number == k)
            def _(item=item, out=out):
                out[...] = item[...]


def near_call(inverted, route, items, after=()):
    return pl.pallas_call(
        functools.partial(near_kernel, inverted),
        in_specs=[IN_SMEM] + [IN_VMEM] * 4 + [pl.BlockSpec(memory_space=pl.ANY)] * len(after),
        out_specs=[IN_VMEM] * 3,
        out_shape=[jax.ShapeDtypeStruct((HEADS, 8, DIM), jnp.float32)] * 3,
        compiler_params=params(8),
        cost_estimate=work(1024, 16 * MIB),
        name="near_rows",
    )(route, *items, *after)


def kept_kernel(targets_ref, *refs):
    items, kept_hbm, sem = refs[:7], refs[7], refs[8]
    number = landing(origin(targets_ref, lax.axis_index("asset")))
    for k, item in enumerate(items):
        @pl.when(number == k)
        def _(item=item):
            copy = pltpu.make_async_copy(item, kept_hbm.at[0], sem)
            copy.start()
            copy.wait()


def kept_call(targets, items):
    return pl.pallas_call(
        kept_kernel,
        in_specs=[IN_SMEM] + [pl.BlockSpec(memory_space=pl.ANY)] * 7,
        out_specs=pl.BlockSpec(memory_space=pl.ANY),
        out_shape=jax.ShapeDtypeStruct((1, HEADS, 8, DIM), jnp.float32),
        scratch_shapes=[DMA],
        compiler_params=params(8),
        cost_estimate=work(1024, 2 ** 17),
        name="kept_rows",
    )(targets, *items)


def swap(value, bits, axis="asset"):
    return lax.ppermute(value, axis, [(k, k ^ bits) for k in range(SHARDS)])


def on_device(tokens, w_query, w_key, w_value, decay_log, lengths, sources, targets, stash, whiten):
    tokens, decay, whiten = tokens[0], decay_log[0], whiten[0]
    own = fetch_call(stash)
    items = [own] + [swap(own, 4 * k) for k in (1, 2, 3)]
    *quarters, keys, values, sums = keys_call(lengths, tokens, w_key, w_value, decay)
    near = near_call(False, sources, items)
    near, quarters = lax.optimization_barrier((near, quarters))
    arrived = [quarters[0]] + [swap(quarters[k], k, "seq") for k in (1, 2, 3)]
    items += [swap(item, k) for k, item in enumerate(near, 1)]
    ordered, payload = row_call(sources, arrived, items)
    payloads = [payload] + [swap(payload, 4 * m, "seq") for m in (1, 2, 3)]
    mixed = inner_call(tokens, w_query, keys, values, sums, payload)
    *carried, closing = carry_call(payloads, ordered, mixed)
    state = [carried[0]] + [swap(carried[k], k, "seq") for k in (1, 2, 3)]
    items = [closing] + [swap(closing, 4 * k) for k in (1, 2, 3)]
    features, mark = outer_call(lengths, mixed, state, whiten)
    near = near_call(True, targets, items, (mark,))
    items += [swap(item, k) for k, item in enumerate(near, 1)]
    return (features[None], kept_call(targets, items))


def solution(mesh):
    return jax.shard_map(
        on_device,
        mesh=mesh,
        in_specs=(
            P("asset", "seq", None),
            P(),
            P(),
            P(),
            P("asset", None, "seq"),
            P("asset"),
            P(),
            P(),
            P("asset", None, "seq", None),
            P("asset", None, None),
        ),
        out_specs=(P("asset", "seq", None), P("asset", None, "seq", None)),
        check_vma=False,
    )
```

```python
import functools
import jax
import jax.numpy as jnp
from jax import lax
from jax.experimental import pallas as pl
from jax.experimental.pallas import tpu as pltpu
from jax.sharding import PartitionSpec as P

HEADS = 8
DIM = 128
STEPS = 512
WIDTH = 1024
PAIR = 2 * DIM
HALF = 256
SHARDS = 16
EPSILON = 1e-05
LOG2E = 1.4426950408889634
FAR = -1e30
MIB = 1024 * 1024
IN_HBM = pl.BlockSpec(memory_space=pltpu.HBM)
IN_VMEM = pl.BlockSpec(memory_space=pltpu.VMEM)
IN_SMEM = pl.BlockSpec(memory_space=pltpu.SMEM)
DMA = pltpu.SemaphoreType.DMA


def lanes_of(number, size=PAIR):
    return slice(number * size, (number + 1) * size)


def params(mib):
    return pltpu.CompilerParams(vmem_limit_bytes=mib * MIB)


def work(flops, nbytes):
    return pl.CostEstimate(flops=flops, bytes_accessed=nbytes, transcendentals=0)


def running_sum(rates):
    lane = lax.broadcasted_iota(jnp.int32, rates.shape, 1)
    shift = 1
    while shift < STEPS:
        moved = pltpu.roll(rates, shift, 1)
        rates = rates + jnp.where(lane >= shift, moved, 0.0)
        shift *= 2
    return rates


def split(state):
    high = state.astype(jnp.bfloat16)
    low = (state - high.astype(jnp.float32)).astype(jnp.bfloat16)
    return jnp.concatenate([high, low], 0)


def turned(sums):
    padding = jnp.zeros((DIM - HEADS, STEPS), jnp.float32)
    return jnp.concatenate([sums, padding], 0).T


def place():
    rank = lax.axis_index("seq")
    return rank & 3, rank >> 2


def mark_kernel(mark_ref):
    mark_ref[...] = jnp.zeros((8, DIM), jnp.float32)


def mark_call():
    return pl.pallas_call(
        mark_kernel,
        out_specs=IN_VMEM,
        out_shape=jax.ShapeDtypeStruct((8, DIM), jnp.float32),
        compiler_params=params(8),
        cost_estimate=pl.CostEstimate(flops=2 ** 36, bytes_accessed=2 ** 30, transcendentals=2 ** 30),
        name="mark",
    )()


def keys_kernel(lengths_ref, tokens_ref, w_key_ref, w_value_ref, decay_ref, *refs):
    quarters = refs[:4]
    keys_ref, values_ref, sums_ref, quarter_ref = refs[4:]
    valid = lengths_ref[0] - lax.axis_index("seq") * STEPS
    lane = lax.broadcasted_iota(jnp.int32, (HEADS, STEPS), 1)
    sums = running_sum(jnp.where(lane < valid, decay_ref[...] * LOG2E, 0.0))
    sums_ref[...] = sums
    growth = jnp.broadcast_to(sums[:, STEPS - 1:], (HEADS, DIM))
    tails = jnp.exp2(sums[:, STEPS - 1:] - sums)
    alive = lax.broadcasted_iota(jnp.int32, (STEPS, PAIR), 0) < valid
    tokens = tokens_ref[...]
    for pair in range(4):
        lanes = lanes_of(pair)
        keys = jnp.dot(tokens, w_key_ref[:, lanes], preferred_element_type=jnp.float32)
        keys_t = jnp.where(alive, keys * DIM ** (-0.5), 0.0).astype(jnp.bfloat16).T
        values = jnp.dot(tokens, w_value_ref[:, lanes], preferred_element_type=jnp.float32)
        values = jnp.where(alive, values, 0.0).astype(jnp.bfloat16)
        keys_ref[lanes, :] = keys_t
        values_ref[:, lanes] = values
        for j in range(2):
            head = 2 * pair + j
            own = lanes_of(j, DIM)
            decayed = (keys_t[own].astype(jnp.float32) * tails[head:head + 1]).astype(jnp.bfloat16)
            total = jnp.dot(decayed, values[:, own], preferred_element_type=jnp.float32)
            for block in range(SHARDS):
                quarter_ref[block % 4, (block // 4) * HEADS + head] = total[block * 8:(block + 1) * 8]
    x, _ = place()
    for k, out in enumerate(quarters):
        out[:32] = quarter_ref[x ^ k]
        out[32] = growth


def keys_call(lengths, tokens, w_key, w_value, decay):
    return pl.pallas_call(
        keys_kernel,
        in_specs=[IN_SMEM] + [IN_VMEM] * 4,
        out_specs=[IN_VMEM] * 7,
        out_shape=[jax.ShapeDtypeStruct((33, 8, DIM), jnp.float32)] * 4 + [
            jax.ShapeDtypeStruct((WIDTH, STEPS), jnp.bfloat16),
            jax.ShapeDtypeStruct((STEPS, WIDTH), jnp.bfloat16),
            jax.ShapeDtypeStruct((HEADS, STEPS), jnp.float32),
        ],
        scratch_shapes=[pltpu.VMEM((4, 32, 8, DIM), jnp.float32)],
        compiler_params=params(16),
        cost_estimate=work(2 * STEPS * WIDTH * WIDTH * 3, 16 * MIB),
        name="keys_values",
    )(lengths, tokens, w_key, w_value, decay)


def inner_kernel(tokens_ref, w_query_ref, keys_ref, values_ref, sums_ref, after_ref, mixed_ref):
    sums = sums_ref[...]
    columns = turned(sums)
    causal = (lax.broadcasted_iota(jnp.int32, (DIM, DIM), 0)
              >= lax.broadcasted_iota(jnp.int32, (DIM, DIM), 1))
    tokens = tokens_ref[...]
    for pair in range(4):
        lanes = lanes_of(pair)
        queries = jnp.dot(tokens, w_query_ref[:, lanes], preferred_element_type=jnp.float32).astype(jnp.bfloat16)
        for j in range(2):
            head = 2 * pair + j
            own = lanes_of(head, DIM)
            attend(causal, sums[head:head + 1], columns[:, head:head + 1], queries[:, lanes_of(j, DIM)],
                   keys_ref[own, :], values_ref[:, own], own, mixed_ref)


def inner_call(tokens, w_query, keys, values, sums, after):
    return pl.pallas_call(
        inner_kernel,
        in_specs=[IN_VMEM] * 5 + [pl.BlockSpec(memory_space=pl.ANY)],
        out_specs=IN_VMEM,
        out_shape=jax.ShapeDtypeStruct((2, STEPS, WIDTH), jnp.bfloat16),
        compiler_params=params(16),
        cost_estimate=work(2 * STEPS * WIDTH * WIDTH * 3, 5 * MIB),
        name="queries_inner",
    )(tokens, w_query, keys, values, sums, after)


def attend(causal, row, column, queries, keys_t, values, own, mixed_ref):
    first = slice(0, HALF)
    middle = row[:, HALF - 1:HALF]
    decayed = (keys_t[:, first].astype(jnp.float32) * jnp.exp2(middle - row[:, first])).astype(jnp.bfloat16)
    state = split(jnp.dot(decayed, values[first], preferred_element_type=jnp.float32))
    column = jnp.broadcast_to(column, (STEPS, DIM))
    mixed_ref[0, :, own] = (queries.astype(jnp.float32) * jnp.exp2(column)).astype(jnp.bfloat16)
    for c in range(2):
        rows = lanes_of(c)
        q = queries[rows]
        scores = jnp.dot(q, keys_t[:, rows], preferred_element_type=jnp.float32)
        strips = []
        for s in range(2):
            here = column[c * HALF + s * DIM:c * HALF + (s + 1) * DIM]
            parts = []
            for b in range(s + 1):
                gap = here - row[:, c * HALF + b * DIM:c * HALF + (b + 1) * DIM]
                if b == s:
                    gap = jnp.where(causal, gap, FAR)
                score = scores[s * DIM:(s + 1) * DIM, b * DIM:(b + 1) * DIM]
                parts.append((score * jnp.exp2(gap)).astype(jnp.bfloat16))
            if s == 0:
                parts.append(jnp.zeros((DIM, DIM), jnp.bfloat16))
            strips.append(jnp.concatenate(parts, 1))
        weights = jnp.concatenate(strips, 0)
        part = jnp.dot(weights, values[rows], preferred_element_type=jnp.float32)
        if c == 1:
            cross = jnp.dot(jnp.concatenate([q, q], 1), state, preferred_element_type=jnp.float32)
            part = part + cross * jnp.exp2(column[HALF:] - middle)
        part = part - jnp.mean(part, axis=1, keepdims=True)
        mixed_ref[1, rows, own] = part.astype(jnp.bfloat16)


def row_kernel(sources_ref, *refs):
    quarters, items = refs[:4], refs[4:11]
    ordered_ref, payload_ref = refs[11:]
    x, _ = place()
    number = landing(lookup(sources_ref, lax.axis_index("asset"), False))
    for k, item in enumerate(items):
        @pl.when(number == k)
        def _(item=item):
            payload_ref[33:41] = item[...]
    for k, quarter in enumerate(quarters):
        ordered_ref[x ^ k] = quarter[...]
    for row in range(32):
        head = row % HEADS
        state = ordered_ref[0, row]
        for shard in range(1, 4):
            state = jnp.exp2(ordered_ref[shard, 32, head:head + 1]) * state + ordered_ref[shard, row]
        payload_ref[row] = state
    growth = ordered_ref[0, 32]
    for shard in range(1, 4):
        growth = growth + ordered_ref[shard, 32]
    payload_ref[32] = growth


def row_call(sources, quarters, items):
    return pl.pallas_call(
        row_kernel,
        in_specs=[IN_VMEM] * 12,
        out_specs=[IN_VMEM] * 2,
        out_shape=[
            jax.ShapeDtypeStruct((4, 33, 8, DIM), jnp.float32),
            jax.ShapeDtypeStruct((41, 8, DIM), jnp.float32),
        ],
        compiler_params=params(8),
        cost_estimate=work(MIB, 16 * MIB),
        name="row_totals",
    )(sources, *quarters, *items)


def carry_kernel(*refs):
    payloads, ordered_ref, carried = refs[:4], refs[4], refs[6:10]
    closing_ref, rows_ref, carry_ref, final_ref = refs[10:]
    x, y = place()
    for m, payload in enumerate(payloads):
        rows_ref[y ^ m] = payload[...]
    for row in range(32):
        head, block = row % HEADS, row // HEADS
        state = rows_ref[block, 33 + head]
        carry = state
        for line in range(4):
            carry = jnp.where(y == line, state, carry)
            state = jnp.exp2(rows_ref[line, 32, head:head + 1]) * state + rows_ref[line, row]
        final_ref[block, head] = state
        carry_ref[0, row] = carry
        for shard in range(3):
            carry = jnp.exp2(ordered_ref[shard, 32, head:head + 1]) * carry + ordered_ref[shard, row]
            carry_ref[shard + 1, row] = carry
    for k, out in enumerate(carried):
        out[...] = carry_ref[x ^ k]
    closing_ref[...] = final_ref[y]


def carry_call(payloads, ordered, after):
    return pl.pallas_call(
        carry_kernel,
        in_specs=[IN_VMEM] * 5 + [pl.BlockSpec(memory_space=pl.ANY)],
        out_specs=[IN_VMEM] * 5,
        out_shape=[jax.ShapeDtypeStruct((32, 8, DIM), jnp.float32)] * 4
        + [jax.ShapeDtypeStruct((HEADS, 8, DIM), jnp.float32)],
        scratch_shapes=[
            pltpu.VMEM((4, 41, 8, DIM), jnp.float32),
            pltpu.VMEM((4, 32, 8, DIM), jnp.float32),
            pltpu.VMEM((4, HEADS, 8, DIM), jnp.float32),
        ],
        compiler_params=params(8),
        cost_estimate=work(MIB, 2 * MIB),
        name="carry_rows",
    )(*payloads, ordered, after)


def norm_kernel(lengths_ref, mixed_ref, *refs):
    quarters, normed_ref, state_ref = refs[:4], *refs[4:]
    x, _ = place()
    for k, quarter in enumerate(quarters):
        for block in range(4):
            state_ref[4 * block + (x ^ k)] = quarter[block * HEADS:(block + 1) * HEADS]
    valid = lengths_ref[0] - lax.axis_index("seq") * STEPS
    same = (lax.broadcasted_iota(jnp.int32, (PAIR, PAIR), 0) // DIM
            == lax.broadcasted_iota(jnp.int32, (PAIR, PAIR), 1) // DIM)
    averaging = jnp.where(same, 1.0 / DIM, 0.0).astype(jnp.bfloat16)
    alive = lax.broadcasted_iota(jnp.int32, (STEPS, PAIR), 0) < valid
    for pair in range(4):
        halves = []
        for head in (2 * pair, 2 * pair + 1):
            own = lanes_of(head, DIM)
            state = state_ref[:, head].reshape(DIM, DIM)
            state = split(state - jnp.mean(state, axis=1, keepdims=True))
            q = mixed_ref[0, :, own]
            cross = jnp.dot(jnp.concatenate([q, q], 1), state, preferred_element_type=jnp.float32)
            halves.append(mixed_ref[1, :, own].astype(jnp.float32) + cross)
        centered = jnp.concatenate(halves, 1)
        squares = (centered * centered).astype(jnp.bfloat16)
        spread = jnp.dot(squares, averaging, preferred_element_type=jnp.float32)
        scale = jnp.where(alive, lax.rsqrt(spread + EPSILON), 0.0)
        normed_ref[:, lanes_of(pair)] = (centered * scale).astype(jnp.bfloat16)


def norm_call(lengths, mixed, quarters):
    return pl.pallas_call(
        norm_kernel,
        in_specs=[IN_SMEM] + [IN_VMEM] * 5,
        out_specs=IN_VMEM,
        out_shape=jax.ShapeDtypeStruct((STEPS, WIDTH), jnp.bfloat16),
        scratch_shapes=[pltpu.VMEM((SHARDS, HEADS, 8, DIM), jnp.float32)],
        compiler_params=params(12),
        cost_estimate=work(2 * STEPS * WIDTH * WIDTH * 2, 4 * MIB),
        name="cross_norm",
    )(lengths, mixed, *quarters)


def whiten_kernel(normed_ref, whiten_ref, after_ref, features_hbm, out_ref, out_sems):
    copies = []
    for part in range(2):
        lanes = lanes_of(part, 512)
        out_ref[:, lanes] = jnp.dot(
            normed_ref[...], whiten_ref[:, lanes], preferred_element_type=jnp.float32).astype(jnp.bfloat16)
        copies.append(pltpu.make_async_copy(out_ref.at[:, lanes], features_hbm.at[:, lanes], out_sems.at[part]))
        copies[part].start()
    for copy in copies:
        copy.wait()


def whiten_call(normed, whiten, after):
    return pl.pallas_call(
        whiten_kernel,
        in_specs=[IN_VMEM] * 2 + [pl.BlockSpec(memory_space=pl.ANY)],
        out_specs=IN_HBM,
        out_shape=jax.ShapeDtypeStruct((STEPS, WIDTH), jnp.bfloat16),
        scratch_shapes=[pltpu.VMEM((STEPS, WIDTH), jnp.bfloat16), DMA((2,))],
        compiler_params=params(12),
        cost_estimate=work(2 * STEPS * WIDTH * WIDTH * 2, 4 * MIB),
        name="whiten_rows",
    )(normed, whiten, after)


def lookup(route_ref, slot, inverted):
    route = route_ref[...].astype(jnp.float32)
    lane = lax.broadcasted_iota(jnp.int32, route.shape, 1).astype(jnp.float32)
    slot = slot.astype(jnp.float32)
    found = jnp.where(route == slot, lane, 0.0) if inverted else jnp.where(lane == slot, route, 0.0)
    return jnp.sum(found).astype(jnp.int32)


def landing(source):
    me = lax.axis_index("asset")
    steps = (me ^ source) & 3
    return jnp.where(steps == 0, (me ^ source) >> 2, 3 + steps)


def near_kernel(inverted, route_ref, *refs):
    items, outs = refs[:4], refs[-3:]
    me = lax.axis_index("asset")
    for j, out in enumerate(outs, 1):
        slot = me ^ j
        source = lookup(route_ref, slot, inverted)
        number = ((me ^ source) >> 2) & 3
        for k, item in enumerate(items):
            @pl.when(number == k)
            def _(item=item, out=out):
                out[...] = item[...]


def near_call(inverted, route, items, after=()):
    return pl.pallas_call(
        functools.partial(near_kernel, inverted),
        in_specs=[IN_VMEM] * 5 + [pl.BlockSpec(memory_space=pl.ANY)] * len(after),
        out_specs=[IN_VMEM] * 3,
        out_shape=[jax.ShapeDtypeStruct((HEADS, 8, DIM), jnp.float32)] * 3,
        compiler_params=params(8),
        cost_estimate=work(1024, 16 * MIB),
        name="near_rows",
    )(route, *items, *after)


def kept_kernel(targets_ref, *refs):
    items, kept_hbm, sem = refs[:7], refs[7], refs[8]
    number = landing(lookup(targets_ref, lax.axis_index("asset"), True))
    for k, item in enumerate(items):
        @pl.when(number == k)
        def _(item=item):
            copy = pltpu.make_async_copy(item, kept_hbm.at[0], sem)
            copy.start()
            copy.wait()


def kept_call(targets, items):
    return pl.pallas_call(
        kept_kernel,
        in_specs=[IN_VMEM] + [pl.BlockSpec(memory_space=pl.ANY)] * 7,
        out_specs=pl.BlockSpec(memory_space=pl.ANY),
        out_shape=jax.ShapeDtypeStruct((1, HEADS, 8, DIM), jnp.float32),
        scratch_shapes=[DMA],
        compiler_params=params(8),
        cost_estimate=work(1024, 2 ** 17),
        name="kept_rows",
    )(targets, *items)


def swap(value, bits, axis="asset"):
    return lax.ppermute(value, axis, [(k, k ^ bits) for k in range(SHARDS)])


def on_device(tokens, w_query, w_key, w_value, decay_log, lengths, sources, targets, stash, whiten):
    tokens, decay, whiten = tokens[0], decay_log[0], whiten[0]
    sources, targets = sources[None], targets[None]
    stash, mark = lax.optimization_barrier((stash, mark_call()))
    own = stash[0]
    items = [own] + [swap(own, 4 * k) for k in (1, 2, 3)]
    *quarters, keys, values, sums = keys_call(lengths, tokens, w_key, w_value, decay)
    near = near_call(False, sources, items, (mark,))
    near, quarters = lax.optimization_barrier((near, quarters))
    moved = {k: swap(quarters[k], k, "seq") for k in (2, 1, 3)}
    arrived = [quarters[0]] + [moved[k] for k in (1, 2, 3)]
    items += [swap(item, k) for k, item in enumerate(near, 1)]
    ordered, payload = row_call(sources, arrived, items)
    moved = {m: swap(payload, 4 * m, "seq") for m in (1, 3, 2)}
    payloads = [payload] + [moved[m] for m in (1, 2, 3)]
    mixed = inner_call(tokens, w_query, keys, values, sums, payload)
    *carried, closing = carry_call(payloads, ordered, mixed)
    moved = {k: swap(carried[k], k, "seq") for k in (2, 1, 3)}
    state = [carried[0]] + [moved[k] for k in (1, 2, 3)]
    items = [closing] + [swap(closing, 4 * k) for k in (1, 2, 3)]
    normed = norm_call(lengths, mixed, state)
    near = near_call(True, targets, items, (normed,))
    items += [swap(item, k) for k, item in enumerate(near, 1)]
    features = whiten_call(normed, whiten, near[0])
    return (features[None], kept_call(targets, items))


def solution(mesh):
    return jax.shard_map(
        on_device,
        mesh=mesh,
        in_specs=(
            P("asset", "seq", None),
            P(),
            P(),
            P(),
            P("asset", None, "seq"),
            P("asset"),
            P(),
            P(),
            P("asset", None, "seq", None),
            P("asset", None, None),
        ),
        out_specs=(P("asset", "seq", None), P("asset", None, "seq", None)),
        check_vma=False,
    )
```

```python
import functools
import jax
import jax.numpy as jnp
from jax import lax
from jax.experimental import pallas as pl
from jax.experimental.pallas import tpu as pltpu
from jax.sharding import PartitionSpec as P

HEADS = 8
DIM = 128
STEPS = 512
WIDTH = 1024
PAIR = 2 * DIM
HALF = 256
SHARDS = 16
EPSILON = 1e-05
LOG2E = 1.4426950408889634
FAR = -1e30
MIB = 1024 * 1024
ROW_ORDER = (0, 2, 1, 3)
LINE_ORDER = (0, 1, 3, 2)
FAR_ORDER = (0, 1, 3, 2, 4, 5, 6)
IN_HBM = pl.BlockSpec(memory_space=pltpu.HBM)
IN_VMEM = pl.BlockSpec(memory_space=pltpu.VMEM)
IN_SMEM = pl.BlockSpec(memory_space=pltpu.SMEM)
DMA = pltpu.SemaphoreType.DMA


def lanes_of(number, size=PAIR):
    return slice(number * size, (number + 1) * size)


def params(mib):
    return pltpu.CompilerParams(vmem_limit_bytes=mib * MIB)


def work(flops, nbytes):
    return pl.CostEstimate(flops=flops, bytes_accessed=nbytes, transcendentals=0)


def running_sum(rates):
    lane = lax.broadcasted_iota(jnp.int32, rates.shape, 1)
    shift = 1
    while shift < STEPS:
        moved = pltpu.roll(rates, shift, 1)
        rates = rates + jnp.where(lane >= shift, moved, 0.0)
        shift *= 2
    return rates


def split(state):
    high = state.astype(jnp.bfloat16)
    low = (state - high.astype(jnp.float32)).astype(jnp.bfloat16)
    return jnp.concatenate([high, low], 0)


def turned(sums):
    padding = jnp.zeros((DIM - HEADS, STEPS), jnp.float32)
    return jnp.concatenate([sums, padding], 0).T


def place():
    rank = lax.axis_index("seq")
    return rank & 3, rank >> 2


def mark_kernel(mark_ref):
    mark_ref[...] = jnp.zeros((8, DIM), jnp.float32)


def mark_call():
    return pl.pallas_call(
        mark_kernel,
        out_specs=IN_VMEM,
        out_shape=jax.ShapeDtypeStruct((8, DIM), jnp.float32),
        compiler_params=params(8),
        cost_estimate=pl.CostEstimate(flops=2 ** 36, bytes_accessed=2 ** 30, transcendentals=2 ** 30),
        name="mark",
    )()


def keys_kernel(lengths_ref, tokens_ref, w_key_ref, w_value_ref, decay_ref, *refs):
    quarters = refs[:4]
    keys_ref, values_ref, sums_ref, quarter_ref = refs[4:]
    valid = lengths_ref[0] - lax.axis_index("seq") * STEPS
    lane = lax.broadcasted_iota(jnp.int32, (HEADS, STEPS), 1)
    sums = running_sum(jnp.where(lane < valid, decay_ref[...] * LOG2E, 0.0))
    sums_ref[...] = sums
    growth = jnp.broadcast_to(sums[:, STEPS - 1:], (HEADS, DIM))
    tails = jnp.exp2(sums[:, STEPS - 1:] - sums)
    alive = lax.broadcasted_iota(jnp.int32, (STEPS, PAIR), 0) < valid
    tokens = tokens_ref[...]
    for pair in range(4):
        lanes = lanes_of(pair)
        keys = jnp.dot(tokens, w_key_ref[:, lanes], preferred_element_type=jnp.float32)
        keys_t = jnp.where(alive, keys * DIM ** (-0.5), 0.0).astype(jnp.bfloat16).T
        values = jnp.dot(tokens, w_value_ref[:, lanes], preferred_element_type=jnp.float32)
        values = jnp.where(alive, values, 0.0).astype(jnp.bfloat16)
        keys_ref[lanes, :] = keys_t
        values_ref[:, lanes] = values
        for j in range(2):
            head = 2 * pair + j
            own = lanes_of(j, DIM)
            decayed = (keys_t[own].astype(jnp.float32) * tails[head:head + 1]).astype(jnp.bfloat16)
            total = jnp.dot(decayed, values[:, own], preferred_element_type=jnp.float32)
            for block in range(SHARDS):
                quarter_ref[block % 4, (block // 4) * HEADS + head] = total[block * 8:(block + 1) * 8]
    x, _ = place()
    for k, out in enumerate(quarters):
        out[:32] = quarter_ref[x ^ k]
        out[32] = growth


def keys_call(lengths, tokens, w_key, w_value, decay):
    return pl.pallas_call(
        keys_kernel,
        in_specs=[IN_SMEM] + [IN_VMEM] * 4,
        out_specs=[IN_VMEM] * 7,
        out_shape=[jax.ShapeDtypeStruct((33, 8, DIM), jnp.float32)] * 4 + [
            jax.ShapeDtypeStruct((WIDTH, STEPS), jnp.bfloat16),
            jax.ShapeDtypeStruct((STEPS, WIDTH), jnp.bfloat16),
            jax.ShapeDtypeStruct((HEADS, STEPS), jnp.float32),
        ],
        scratch_shapes=[pltpu.VMEM((4, 32, 8, DIM), jnp.float32)],
        compiler_params=params(16),
        cost_estimate=work(2 * STEPS * WIDTH * WIDTH * 3, 16 * MIB),
        name="keys_values",
    )(lengths, tokens, w_key, w_value, decay)


def inner_kernel(tokens_ref, w_query_ref, keys_ref, values_ref, sums_ref, after_ref, mixed_ref):
    sums = sums_ref[...]
    columns = turned(sums)
    causal = (lax.broadcasted_iota(jnp.int32, (DIM, DIM), 0)
              >= lax.broadcasted_iota(jnp.int32, (DIM, DIM), 1))
    tokens = tokens_ref[...]
    for pair in range(4):
        lanes = lanes_of(pair)
        queries = jnp.dot(tokens, w_query_ref[:, lanes], preferred_element_type=jnp.float32).astype(jnp.bfloat16)
        for j in range(2):
            head = 2 * pair + j
            own = lanes_of(head, DIM)
            attend(causal, sums[head:head + 1], columns[:, head:head + 1], queries[:, lanes_of(j, DIM)],
                   keys_ref[own, :], values_ref[:, own], own, mixed_ref)


def inner_call(tokens, w_query, keys, values, sums, after):
    return pl.pallas_call(
        inner_kernel,
        in_specs=[IN_VMEM] * 5 + [pl.BlockSpec(memory_space=pl.ANY)],
        out_specs=IN_VMEM,
        out_shape=jax.ShapeDtypeStruct((2, STEPS, WIDTH), jnp.bfloat16),
        compiler_params=params(16),
        cost_estimate=work(2 * STEPS * WIDTH * WIDTH * 3, 5 * MIB),
        name="queries_inner",
    )(tokens, w_query, keys, values, sums, after)


def attend(causal, row, column, queries, keys_t, values, own, mixed_ref):
    first = slice(0, HALF)
    middle = row[:, HALF - 1:HALF]
    decayed = (keys_t[:, first].astype(jnp.float32) * jnp.exp2(middle - row[:, first])).astype(jnp.bfloat16)
    state = split(jnp.dot(decayed, values[first], preferred_element_type=jnp.float32))
    column = jnp.broadcast_to(column, (STEPS, DIM))
    mixed_ref[0, :, own] = (queries.astype(jnp.float32) * jnp.exp2(column)).astype(jnp.bfloat16)
    for c in range(2):
        rows = lanes_of(c)
        q = queries[rows]
        scores = jnp.dot(q, keys_t[:, rows], preferred_element_type=jnp.float32)
        strips = []
        for s in range(2):
            here = column[c * HALF + s * DIM:c * HALF + (s + 1) * DIM]
            parts = []
            for b in range(s + 1):
                gap = here - row[:, c * HALF + b * DIM:c * HALF + (b + 1) * DIM]
                if b == s:
                    gap = jnp.where(causal, gap, FAR)
                score = scores[s * DIM:(s + 1) * DIM, b * DIM:(b + 1) * DIM]
                parts.append((score * jnp.exp2(gap)).astype(jnp.bfloat16))
            if s == 0:
                parts.append(jnp.zeros((DIM, DIM), jnp.bfloat16))
            strips.append(jnp.concatenate(parts, 1))
        weights = jnp.concatenate(strips, 0)
        part = jnp.dot(weights, values[rows], preferred_element_type=jnp.float32)
        if c == 1:
            cross = jnp.dot(jnp.concatenate([q, q], 1), state, preferred_element_type=jnp.float32)
            part = part + cross * jnp.exp2(column[HALF:] - middle)
        part = part - jnp.mean(part, axis=1, keepdims=True)
        mixed_ref[1, rows, own] = part.astype(jnp.bfloat16)


def row_kernel(sources_ref, *refs):
    quarters, items = refs[:4], refs[4:11]
    ordered_ref, payload_ref = refs[11:]
    x, _ = place()
    number = landing(lookup(sources_ref, lax.axis_index("asset"), False))
    for k, item in zip(FAR_ORDER, items):
        @pl.when(number == k)
        def _(item=item):
            payload_ref[33:41] = item[...]
    for k, quarter in zip(ROW_ORDER, quarters):
        ordered_ref[x ^ k] = quarter[...]
    for row in range(32):
        head = row % HEADS
        state = ordered_ref[0, row]
        for shard in range(1, 4):
            state = jnp.exp2(ordered_ref[shard, 32, head:head + 1]) * state + ordered_ref[shard, row]
        payload_ref[row] = state
    growth = ordered_ref[0, 32]
    for shard in range(1, 4):
        growth = growth + ordered_ref[shard, 32]
    payload_ref[32] = growth


def row_call(sources, quarters, items):
    return pl.pallas_call(
        row_kernel,
        in_specs=[IN_VMEM] * 12,
        out_specs=[IN_VMEM] * 2,
        out_shape=[
            jax.ShapeDtypeStruct((4, 33, 8, DIM), jnp.float32),
            jax.ShapeDtypeStruct((41, 8, DIM), jnp.float32),
        ],
        compiler_params=params(8),
        cost_estimate=work(MIB, 16 * MIB),
        name="row_totals",
    )(sources, *quarters, *items)


def carry_kernel(*refs):
    payloads, ordered_ref, carried = refs[:4], refs[4], refs[6:10]
    closing_ref, rows_ref, carry_ref, final_ref = refs[10:]
    x, y = place()
    for m, payload in zip(LINE_ORDER, payloads):
        rows_ref[y ^ m] = payload[...]
    for row in range(32):
        head, block = row % HEADS, row // HEADS
        state = rows_ref[block, 33 + head]
        carry = state
        for line in range(4):
            carry = jnp.where(y == line, state, carry)
            state = jnp.exp2(rows_ref[line, 32, head:head + 1]) * state + rows_ref[line, row]
        final_ref[block, head] = state
        carry_ref[0, row] = carry
        for shard in range(3):
            carry = jnp.exp2(ordered_ref[shard, 32, head:head + 1]) * carry + ordered_ref[shard, row]
            carry_ref[shard + 1, row] = carry
    for k, out in enumerate(carried):
        out[...] = carry_ref[x ^ k]
    closing_ref[...] = final_ref[y]


def carry_call(payloads, ordered, after):
    return pl.pallas_call(
        carry_kernel,
        in_specs=[IN_VMEM] * 5 + [pl.BlockSpec(memory_space=pl.ANY)],
        out_specs=[IN_VMEM] * 5,
        out_shape=[jax.ShapeDtypeStruct((32, 8, DIM), jnp.float32)] * 4
        + [jax.ShapeDtypeStruct((HEADS, 8, DIM), jnp.float32)],
        scratch_shapes=[
            pltpu.VMEM((4, 41, 8, DIM), jnp.float32),
            pltpu.VMEM((4, 32, 8, DIM), jnp.float32),
            pltpu.VMEM((4, HEADS, 8, DIM), jnp.float32),
        ],
        compiler_params=params(8),
        cost_estimate=work(MIB, 2 * MIB),
        name="carry_rows",
    )(*payloads, ordered, after)


def norm_kernel(lengths_ref, mixed_ref, *refs):
    quarters, normed_ref, state_ref = refs[:4], *refs[4:]
    x, _ = place()
    for k, quarter in zip(ROW_ORDER, quarters):
        for block in range(4):
            state_ref[4 * block + (x ^ k)] = quarter[block * HEADS:(block + 1) * HEADS]
    valid = lengths_ref[0] - lax.axis_index("seq") * STEPS
    same = (lax.broadcasted_iota(jnp.int32, (PAIR, PAIR), 0) // DIM
            == lax.broadcasted_iota(jnp.int32, (PAIR, PAIR), 1) // DIM)
    averaging = jnp.where(same, 1.0 / DIM, 0.0).astype(jnp.bfloat16)
    alive = lax.broadcasted_iota(jnp.int32, (STEPS, PAIR), 0) < valid
    for pair in range(4):
        halves = []
        for head in (2 * pair, 2 * pair + 1):
            own = lanes_of(head, DIM)
            state = state_ref[:, head].reshape(DIM, DIM)
            state = split(state - jnp.mean(state, axis=1, keepdims=True))
            q = mixed_ref[0, :, own]
            cross = jnp.dot(jnp.concatenate([q, q], 1), state, preferred_element_type=jnp.float32)
            halves.append(mixed_ref[1, :, own].astype(jnp.float32) + cross)
        centered = jnp.concatenate(halves, 1)
        squares = (centered * centered).astype(jnp.bfloat16)
        spread = jnp.dot(squares, averaging, preferred_element_type=jnp.float32)
        scale = jnp.where(alive, lax.rsqrt(spread + EPSILON), 0.0)
        normed_ref[:, lanes_of(pair)] = (centered * scale).astype(jnp.bfloat16)


def norm_call(lengths, mixed, quarters):
    return pl.pallas_call(
        norm_kernel,
        in_specs=[IN_SMEM] + [IN_VMEM] * 5,
        out_specs=IN_VMEM,
        out_shape=jax.ShapeDtypeStruct((STEPS, WIDTH), jnp.bfloat16),
        scratch_shapes=[pltpu.VMEM((SHARDS, HEADS, 8, DIM), jnp.float32)],
        compiler_params=params(12),
        cost_estimate=work(2 * STEPS * WIDTH * WIDTH * 2, 4 * MIB),
        name="cross_norm",
    )(lengths, mixed, *quarters)


def whiten_kernel(normed_ref, whiten_ref, after_ref, features_hbm, out_ref, out_sems):
    copies = []
    for part in range(2):
        lanes = lanes_of(part, 512)
        out_ref[:, lanes] = jnp.dot(
            normed_ref[...], whiten_ref[:, lanes], preferred_element_type=jnp.float32).astype(jnp.bfloat16)
        copies.append(pltpu.make_async_copy(out_ref.at[:, lanes], features_hbm.at[:, lanes], out_sems.at[part]))
        copies[part].start()
    for copy in copies:
        copy.wait()


def whiten_call(normed, whiten, after):
    return pl.pallas_call(
        whiten_kernel,
        in_specs=[IN_VMEM] * 2 + [pl.BlockSpec(memory_space=pl.ANY)],
        out_specs=IN_HBM,
        out_shape=jax.ShapeDtypeStruct((STEPS, WIDTH), jnp.bfloat16),
        scratch_shapes=[pltpu.VMEM((STEPS, WIDTH), jnp.bfloat16), DMA((2,))],
        compiler_params=params(12),
        cost_estimate=work(2 * STEPS * WIDTH * WIDTH * 2, 4 * MIB),
        name="whiten_rows",
    )(normed, whiten, after)


def lookup(route_ref, slot, inverted):
    route = route_ref[...].astype(jnp.float32)
    lane = lax.broadcasted_iota(jnp.int32, route.shape, 1).astype(jnp.float32)
    slot = slot.astype(jnp.float32)
    found = jnp.where(route == slot, lane, 0.0) if inverted else jnp.where(lane == slot, route, 0.0)
    return jnp.sum(found).astype(jnp.int32)


def landing(source):
    me = lax.axis_index("asset")
    steps = (me ^ source) & 3
    return jnp.where(steps == 0, (me ^ source) >> 2, 3 + steps)


def near_kernel(inverted, route_ref, *refs):
    items, outs = refs[:4], refs[-3:]
    me = lax.axis_index("asset")
    for j, out in enumerate(outs, 1):
        slot = me ^ j
        source = lookup(route_ref, slot, inverted)
        number = ((me ^ source) >> 2) & 3
        for k, item in zip(FAR_ORDER, items):
            @pl.when(number == k)
            def _(item=item, out=out):
                out[...] = item[...]


def near_call(inverted, route, items, after=()):
    return pl.pallas_call(
        functools.partial(near_kernel, inverted),
        in_specs=[IN_VMEM] * 5 + [pl.BlockSpec(memory_space=pl.ANY)] * len(after),
        out_specs=[IN_VMEM] * 3,
        out_shape=[jax.ShapeDtypeStruct((HEADS, 8, DIM), jnp.float32)] * 3,
        compiler_params=params(8),
        cost_estimate=work(1024, 16 * MIB),
        name="near_rows",
    )(route, *items, *after)


def kept_kernel(targets_ref, *refs):
    items, kept_hbm, sem = refs[:7], refs[7], refs[8]
    number = landing(lookup(targets_ref, lax.axis_index("asset"), True))
    for k, item in zip(FAR_ORDER, items):
        @pl.when(number == k)
        def _(item=item):
            copy = pltpu.make_async_copy(item, kept_hbm.at[0], sem)
            copy.start()
            copy.wait()


def kept_call(targets, items):
    return pl.pallas_call(
        kept_kernel,
        in_specs=[IN_VMEM] + [pl.BlockSpec(memory_space=pl.ANY)] * 7,
        out_specs=pl.BlockSpec(memory_space=pl.ANY),
        out_shape=jax.ShapeDtypeStruct((1, HEADS, 8, DIM), jnp.float32),
        scratch_shapes=[DMA],
        compiler_params=params(8),
        cost_estimate=work(1024, 2 ** 17),
        name="kept_rows",
    )(targets, *items)


def swap(value, bits, axis="asset"):
    return lax.ppermute(value, axis, [(k, k ^ bits) for k in range(SHARDS)])


def on_device(tokens, w_query, w_key, w_value, decay_log, lengths, sources, targets, stash, whiten):
    tokens, decay, whiten = tokens[0], decay_log[0], whiten[0]
    sources, targets = sources[None], targets[None]
    stash, mark = lax.optimization_barrier((stash, mark_call()))
    own = stash[0]
    items = [own] + [swap(own, 4 * k) for k in FAR_ORDER[1:4]]
    *quarters, keys, values, sums = keys_call(lengths, tokens, w_key, w_value, decay)
    near = near_call(False, sources, items, (mark,))
    near, quarters = lax.optimization_barrier((near, quarters))
    arrived = [quarters[0]] + [swap(quarters[k], k, "seq") for k in ROW_ORDER[1:]]
    items += [swap(item, k) for k, item in enumerate(near, 1)]
    ordered, payload = row_call(sources, arrived, items)
    payloads = [payload] + [swap(payload, 4 * m, "seq") for m in LINE_ORDER[1:]]
    mixed = inner_call(tokens, w_query, keys, values, sums, payload)
    *carried, closing = carry_call(payloads, ordered, mixed)
    state = [carried[0]] + [swap(carried[k], k, "seq") for k in ROW_ORDER[1:]]
    items = [closing] + [swap(closing, 4 * k) for k in FAR_ORDER[1:4]]
    normed = norm_call(lengths, mixed, state)
    near = near_call(True, targets, items, (normed,))
    items += [swap(item, k) for k, item in enumerate(near, 1)]
    features = whiten_call(normed, whiten, near[0])
    return (features[None], kept_call(targets, items))


def solution(mesh):
    return jax.shard_map(
        on_device,
        mesh=mesh,
        in_specs=(
            P("asset", "seq", None),
            P(),
            P(),
            P(),
            P("asset", None, "seq"),
            P("asset"),
            P(),
            P(),
            P("asset", None, "seq", None),
            P("asset", None, None),
        ),
        out_specs=(P("asset", "seq", None), P("asset", None, "seq", None)),
        check_vma=False,
    )
```

```python
import functools
import jax
import jax.numpy as jnp
from jax import lax
from jax.experimental import pallas as pl
from jax.experimental.pallas import tpu as pltpu
from jax.sharding import PartitionSpec as P

HEADS = 8
DIM = 128
STEPS = 512
WIDTH = 1024
PAIR = 2 * DIM
HALF = 256
SHARDS = 16
EPSILON = 1e-05
LOG2E = 1.4426950408889634
FAR = -1e30
MIB = 1024 * 1024
ROW_ORDER = (0, 2, 1, 3)
LINE_ORDER = (0, 3, 1, 2)
FAR_ORDER = (0, 1, 3, 2, 4, 5, 6)
START_ORDER = (0, 1, 3, 2, 6, 5, 4)
IN_HBM = pl.BlockSpec(memory_space=pltpu.HBM)
IN_VMEM = pl.BlockSpec(memory_space=pltpu.VMEM)
IN_SMEM = pl.BlockSpec(memory_space=pltpu.SMEM)
DMA = pltpu.SemaphoreType.DMA


def lanes_of(number, size=PAIR):
    return slice(number * size, (number + 1) * size)


def params(mib):
    return pltpu.CompilerParams(vmem_limit_bytes=mib * MIB)


def work(flops, nbytes):
    return pl.CostEstimate(flops=flops, bytes_accessed=nbytes, transcendentals=0)


def running_sum(rates):
    lane = lax.broadcasted_iota(jnp.int32, rates.shape, 1)
    shift = 1
    while shift < STEPS:
        moved = pltpu.roll(rates, shift, 1)
        rates = rates + jnp.where(lane >= shift, moved, 0.0)
        shift *= 2
    return rates


def split(state):
    high = state.astype(jnp.bfloat16)
    low = (state - high.astype(jnp.float32)).astype(jnp.bfloat16)
    return jnp.concatenate([high, low], 0)


def turned(sums):
    padding = jnp.zeros((DIM - HEADS, STEPS), jnp.float32)
    return jnp.concatenate([sums, padding], 0).T


def place():
    rank = lax.axis_index("seq")
    return rank & 3, rank >> 2


def mark_kernel(mark_ref):
    mark_ref[...] = jnp.zeros((8, DIM), jnp.float32)


def mark_call():
    return pl.pallas_call(
        mark_kernel,
        out_specs=IN_VMEM,
        out_shape=jax.ShapeDtypeStruct((8, DIM), jnp.float32),
        compiler_params=params(8),
        cost_estimate=pl.CostEstimate(flops=2 ** 36, bytes_accessed=2 ** 30, transcendentals=2 ** 30),
        name="mark",
    )()


def keys_kernel(lengths_ref, tokens_ref, w_key_ref, w_value_ref, decay_ref, *refs):
    quarters = refs[:4]
    keys_ref, values_ref, sums_ref, quarter_ref = refs[4:]
    valid = lengths_ref[0] - lax.axis_index("seq") * STEPS
    lane = lax.broadcasted_iota(jnp.int32, (HEADS, STEPS), 1)
    sums = running_sum(jnp.where(lane < valid, decay_ref[...] * LOG2E, 0.0))
    sums_ref[...] = sums
    growth = jnp.broadcast_to(sums[:, STEPS - 1:], (HEADS, DIM))
    tails = jnp.exp2(sums[:, STEPS - 1:] - sums)
    alive = lax.broadcasted_iota(jnp.int32, (STEPS, PAIR), 0) < valid
    tokens = tokens_ref[...]
    for pair in range(4):
        lanes = lanes_of(pair)
        keys = jnp.dot(tokens, w_key_ref[:, lanes], preferred_element_type=jnp.float32)
        keys_t = jnp.where(alive, keys * DIM ** (-0.5), 0.0).astype(jnp.bfloat16).T
        values = jnp.dot(tokens, w_value_ref[:, lanes], preferred_element_type=jnp.float32)
        values = jnp.where(alive, values, 0.0).astype(jnp.bfloat16)
        keys_ref[lanes, :] = keys_t
        values_ref[:, lanes] = values
        for j in range(2):
            head = 2 * pair + j
            own = lanes_of(j, DIM)
            decayed = (keys_t[own].astype(jnp.float32) * tails[head:head + 1]).astype(jnp.bfloat16)
            total = jnp.dot(decayed, values[:, own], preferred_element_type=jnp.float32)
            for block in range(SHARDS):
                quarter_ref[block % 4, (block // 4) * HEADS + head] = total[block * 8:(block + 1) * 8]
    x, _ = place()
    for k, out in enumerate(quarters):
        out[:32] = quarter_ref[x ^ k]
        out[32] = growth


def keys_call(lengths, tokens, w_key, w_value, decay):
    return pl.pallas_call(
        keys_kernel,
        in_specs=[IN_SMEM] + [IN_VMEM] * 4,
        out_specs=[IN_VMEM] * 7,
        out_shape=[jax.ShapeDtypeStruct((33, 8, DIM), jnp.float32)] * 4 + [
            jax.ShapeDtypeStruct((WIDTH, STEPS), jnp.bfloat16),
            jax.ShapeDtypeStruct((STEPS, WIDTH), jnp.bfloat16),
            jax.ShapeDtypeStruct((HEADS, STEPS), jnp.float32),
        ],
        scratch_shapes=[pltpu.VMEM((4, 32, 8, DIM), jnp.float32)],
        compiler_params=params(16),
        cost_estimate=work(2 * STEPS * WIDTH * WIDTH * 3, 16 * MIB),
        name="keys_values",
    )(lengths, tokens, w_key, w_value, decay)


def inner_kernel(tokens_ref, w_query_ref, keys_ref, values_ref, sums_ref, after_ref, mixed_ref):
    sums = sums_ref[...]
    columns = turned(sums)
    causal = (lax.broadcasted_iota(jnp.int32, (DIM, DIM), 0)
              >= lax.broadcasted_iota(jnp.int32, (DIM, DIM), 1))
    tokens = tokens_ref[...]
    for pair in range(4):
        lanes = lanes_of(pair)
        queries = jnp.dot(tokens, w_query_ref[:, lanes], preferred_element_type=jnp.float32).astype(jnp.bfloat16)
        for j in range(2):
            head = 2 * pair + j
            own = lanes_of(head, DIM)
            attend(causal, sums[head:head + 1], columns[:, head:head + 1], queries[:, lanes_of(j, DIM)],
                   keys_ref[own, :], values_ref[:, own], own, mixed_ref)


def inner_call(tokens, w_query, keys, values, sums, after):
    return pl.pallas_call(
        inner_kernel,
        in_specs=[IN_VMEM] * 5 + [pl.BlockSpec(memory_space=pl.ANY)],
        out_specs=IN_VMEM,
        out_shape=jax.ShapeDtypeStruct((2, STEPS, WIDTH), jnp.bfloat16),
        compiler_params=params(16),
        cost_estimate=work(2 * STEPS * WIDTH * WIDTH * 3, 5 * MIB),
        name="queries_inner",
    )(tokens, w_query, keys, values, sums, after)


def attend(causal, row, column, queries, keys_t, values, own, mixed_ref):
    first = slice(0, HALF)
    middle = row[:, HALF - 1:HALF]
    decayed = (keys_t[:, first].astype(jnp.float32) * jnp.exp2(middle - row[:, first])).astype(jnp.bfloat16)
    state = split(jnp.dot(decayed, values[first], preferred_element_type=jnp.float32))
    column = jnp.broadcast_to(column, (STEPS, DIM))
    mixed_ref[0, :, own] = (queries.astype(jnp.float32) * jnp.exp2(column)).astype(jnp.bfloat16)
    for c in range(2):
        rows = lanes_of(c)
        q = queries[rows]
        scores = jnp.dot(q, keys_t[:, rows], preferred_element_type=jnp.float32)
        strips = []
        for s in range(2):
            here = column[c * HALF + s * DIM:c * HALF + (s + 1) * DIM]
            parts = []
            for b in range(s + 1):
                gap = here - row[:, c * HALF + b * DIM:c * HALF + (b + 1) * DIM]
                if b == s:
                    gap = jnp.where(causal, gap, FAR)
                score = scores[s * DIM:(s + 1) * DIM, b * DIM:(b + 1) * DIM]
                parts.append((score * jnp.exp2(gap)).astype(jnp.bfloat16))
            if s == 0:
                parts.append(jnp.zeros((DIM, DIM), jnp.bfloat16))
            strips.append(jnp.concatenate(parts, 1))
        weights = jnp.concatenate(strips, 0)
        part = jnp.dot(weights, values[rows], preferred_element_type=jnp.float32)
        if c == 1:
            cross = jnp.dot(jnp.concatenate([q, q], 1), state, preferred_element_type=jnp.float32)
            part = part + cross * jnp.exp2(column[HALF:] - middle)
        part = part - jnp.mean(part, axis=1, keepdims=True)
        mixed_ref[1, rows, own] = part.astype(jnp.bfloat16)


def row_kernel(sources_ref, *refs):
    quarters, items = refs[:4], refs[4:11]
    ordered_ref, payload_ref = refs[11:]
    x, _ = place()
    number = landing(lookup(sources_ref, lax.axis_index("asset"), False))
    for k, item in zip(START_ORDER, items):
        @pl.when(number == k)
        def _(item=item):
            payload_ref[33:41] = item[...]
    for k, quarter in zip(ROW_ORDER, quarters):
        ordered_ref[x ^ k] = quarter[...]
    for row in range(32):
        head = row % HEADS
        state = ordered_ref[0, row]
        for shard in range(1, 4):
            state = jnp.exp2(ordered_ref[shard, 32, head:head + 1]) * state + ordered_ref[shard, row]
        payload_ref[row] = state
    growth = ordered_ref[0, 32]
    for shard in range(1, 4):
        growth = growth + ordered_ref[shard, 32]
    payload_ref[32] = growth


def row_call(sources, quarters, items):
    return pl.pallas_call(
        row_kernel,
        in_specs=[IN_VMEM] * 12,
        out_specs=[IN_VMEM] * 2,
        out_shape=[
            jax.ShapeDtypeStruct((4, 33, 8, DIM), jnp.float32),
            jax.ShapeDtypeStruct((41, 8, DIM), jnp.float32),
        ],
        compiler_params=params(8),
        cost_estimate=work(MIB, 16 * MIB),
        name="row_totals",
    )(sources, *quarters, *items)


def carry_kernel(*refs):
    payloads, ordered_ref, carried = refs[:4], refs[4], refs[6:10]
    closing_ref, rows_ref, carry_ref, final_ref = refs[10:]
    x, y = place()
    for m, payload in zip(LINE_ORDER, payloads):
        rows_ref[y ^ m] = payload[...]
    for row in range(32):
        head, block = row % HEADS, row // HEADS
        state = rows_ref[block, 33 + head]
        carry = state
        for line in range(4):
            carry = jnp.where(y == line, state, carry)
            state = jnp.exp2(rows_ref[line, 32, head:head + 1]) * state + rows_ref[line, row]
        final_ref[block, head] = state
        carry_ref[0, row] = carry
        for shard in range(3):
            carry = jnp.exp2(ordered_ref[shard, 32, head:head + 1]) * carry + ordered_ref[shard, row]
            carry_ref[shard + 1, row] = carry
    for k, out in enumerate(carried):
        out[...] = carry_ref[x ^ k]
    closing_ref[...] = final_ref[y]


def carry_call(payloads, ordered, after):
    return pl.pallas_call(
        carry_kernel,
        in_specs=[IN_VMEM] * 5 + [pl.BlockSpec(memory_space=pl.ANY)],
        out_specs=[IN_VMEM] * 5,
        out_shape=[jax.ShapeDtypeStruct((32, 8, DIM), jnp.float32)] * 4
        + [jax.ShapeDtypeStruct((HEADS, 8, DIM), jnp.float32)],
        scratch_shapes=[
            pltpu.VMEM((4, 41, 8, DIM), jnp.float32),
            pltpu.VMEM((4, 32, 8, DIM), jnp.float32),
            pltpu.VMEM((4, HEADS, 8, DIM), jnp.float32),
        ],
        compiler_params=params(8),
        cost_estimate=work(MIB, 2 * MIB),
        name="carry_rows",
    )(*payloads, ordered, after)


def norm_kernel(lengths_ref, mixed_ref, *refs):
    quarters, normed_ref, state_ref = refs[:4], *refs[4:]
    x, _ = place()
    for k, quarter in zip(ROW_ORDER, quarters):
        for block in range(4):
            state_ref[4 * block + (x ^ k)] = quarter[block * HEADS:(block + 1) * HEADS]
    valid = lengths_ref[0] - lax.axis_index("seq") * STEPS
    same = (lax.broadcasted_iota(jnp.int32, (PAIR, PAIR), 0) // DIM
            == lax.broadcasted_iota(jnp.int32, (PAIR, PAIR), 1) // DIM)
    averaging = jnp.where(same, 1.0 / DIM, 0.0).astype(jnp.bfloat16)
    alive = lax.broadcasted_iota(jnp.int32, (STEPS, PAIR), 0) < valid
    for pair in range(4):
        halves = []
        for head in (2 * pair, 2 * pair + 1):
            own = lanes_of(head, DIM)
            state = state_ref[:, head].reshape(DIM, DIM)
            state = split(state - jnp.mean(state, axis=1, keepdims=True))
            q = mixed_ref[0, :, own]
            cross = jnp.dot(jnp.concatenate([q, q], 1), state, preferred_element_type=jnp.float32)
            halves.append(mixed_ref[1, :, own].astype(jnp.float32) + cross)
        centered = jnp.concatenate(halves, 1)
        squares = (centered * centered).astype(jnp.bfloat16)
        spread = jnp.dot(squares, averaging, preferred_element_type=jnp.float32)
        scale = jnp.where(alive, lax.rsqrt(spread + EPSILON), 0.0)
        normed_ref[:, lanes_of(pair)] = (centered * scale).astype(jnp.bfloat16)


def norm_call(lengths, mixed, quarters):
    return pl.pallas_call(
        norm_kernel,
        in_specs=[IN_SMEM] + [IN_VMEM] * 5,
        out_specs=IN_VMEM,
        out_shape=jax.ShapeDtypeStruct((STEPS, WIDTH), jnp.bfloat16),
        scratch_shapes=[pltpu.VMEM((SHARDS, HEADS, 8, DIM), jnp.float32)],
        compiler_params=params(12),
        cost_estimate=work(2 * STEPS * WIDTH * WIDTH * 2, 4 * MIB),
        name="cross_norm",
    )(lengths, mixed, *quarters)


def whiten_kernel(normed_ref, whiten_ref, after_ref, features_hbm, out_ref, out_sems):
    copies = []
    for part in range(2):
        lanes = lanes_of(part, 512)
        out_ref[:, lanes] = jnp.dot(
            normed_ref[...], whiten_ref[:, lanes], preferred_element_type=jnp.float32).astype(jnp.bfloat16)
        copies.append(pltpu.make_async_copy(out_ref.at[:, lanes], features_hbm.at[:, lanes], out_sems.at[part]))
        copies[part].start()
    for copy in copies:
        copy.wait()


def whiten_call(normed, whiten, after):
    return pl.pallas_call(
        whiten_kernel,
        in_specs=[IN_VMEM] * 2 + [pl.BlockSpec(memory_space=pl.ANY)],
        out_specs=IN_HBM,
        out_shape=jax.ShapeDtypeStruct((STEPS, WIDTH), jnp.bfloat16),
        scratch_shapes=[pltpu.VMEM((STEPS, WIDTH), jnp.bfloat16), DMA((2,))],
        compiler_params=params(12),
        cost_estimate=work(2 * STEPS * WIDTH * WIDTH * 2, 4 * MIB),
        name="whiten_rows",
    )(normed, whiten, after)


def lookup(route_ref, slot, inverted):
    route = route_ref[...].astype(jnp.float32)
    lane = lax.broadcasted_iota(jnp.int32, route.shape, 1).astype(jnp.float32)
    slot = slot.astype(jnp.float32)
    found = jnp.where(route == slot, lane, 0.0) if inverted else jnp.where(lane == slot, route, 0.0)
    return jnp.sum(found).astype(jnp.int32)


def landing(source):
    me = lax.axis_index("asset")
    steps = (me ^ source) & 3
    return jnp.where(steps == 0, (me ^ source) >> 2, 3 + steps)


def near_kernel(inverted, route_ref, *refs):
    items, outs = refs[:4], refs[-3:]
    me = lax.axis_index("asset")
    for j, out in enumerate(outs, 1):
        slot = me ^ j
        source = lookup(route_ref, slot, inverted)
        number = ((me ^ source) >> 2) & 3
        for k, item in zip(FAR_ORDER, items):
            @pl.when(number == k)
            def _(item=item, out=out):
                out[...] = item[...]


def near_call(inverted, route, items, after=()):
    return pl.pallas_call(
        functools.partial(near_kernel, inverted),
        in_specs=[IN_VMEM] * 5 + [pl.BlockSpec(memory_space=pl.ANY)] * len(after),
        out_specs=[IN_VMEM] * 3,
        out_shape=[jax.ShapeDtypeStruct((HEADS, 8, DIM), jnp.float32)] * 3,
        compiler_params=params(8),
        cost_estimate=work(1024, 16 * MIB),
        name="near_rows",
    )(route, *items, *after)


def kept_kernel(targets_ref, *refs):
    items, kept_hbm, sem = refs[:7], refs[7], refs[8]
    number = landing(lookup(targets_ref, lax.axis_index("asset"), True))
    for k, item in zip(FAR_ORDER, items):
        @pl.when(number == k)
        def _(item=item):
            copy = pltpu.make_async_copy(item, kept_hbm.at[0], sem)
            copy.start()
            copy.wait()


def kept_call(targets, items):
    return pl.pallas_call(
        kept_kernel,
        in_specs=[IN_VMEM] + [pl.BlockSpec(memory_space=pl.ANY)] * 7,
        out_specs=pl.BlockSpec(memory_space=pl.ANY),
        out_shape=jax.ShapeDtypeStruct((1, HEADS, 8, DIM), jnp.float32),
        scratch_shapes=[DMA],
        compiler_params=params(8),
        cost_estimate=work(1024, 2 ** 17),
        name="kept_rows",
    )(targets, *items)


def swap(value, bits, axis="asset"):
    return lax.ppermute(value, axis, [(k, k ^ bits) for k in range(SHARDS)])


def on_device(tokens, w_query, w_key, w_value, decay_log, lengths, sources, targets, stash, whiten):
    tokens, decay, whiten = tokens[0], decay_log[0], whiten[0]
    sources, targets = sources[None], targets[None]
    stash, mark = lax.optimization_barrier((stash, mark_call()))
    own = stash[0]
    items = [own] + [swap(own, 4 * k) for k in FAR_ORDER[1:4]]
    *quarters, keys, values, sums = keys_call(lengths, tokens, w_key, w_value, decay)
    near = near_call(False, sources, items, (mark,))
    near, quarters = lax.optimization_barrier((near, quarters))
    arrived = [quarters[0]] + [swap(quarters[k], k, "seq") for k in ROW_ORDER[1:]]
    items += [swap(near[k - 1], k) for k in (3, 2, 1)]
    ordered, payload = row_call(sources, arrived, items)
    payloads = [payload] + [swap(payload, 4 * m, "seq") for m in LINE_ORDER[1:]]
    mixed = inner_call(tokens, w_query, keys, values, sums, payload)
    *carried, closing = carry_call(payloads, ordered, mixed)
    state = [carried[0]] + [swap(carried[k], k, "seq") for k in ROW_ORDER[1:]]
    items = [closing] + [swap(closing, 4 * k) for k in FAR_ORDER[1:4]]
    normed = norm_call(lengths, mixed, state)
    near = near_call(True, targets, items, (normed,))
    items += [swap(item, k) for k, item in enumerate(near, 1)]
    features = whiten_call(normed, whiten, near[0])
    return (features[None], kept_call(targets, items))


def solution(mesh):
    return jax.shard_map(
        on_device,
        mesh=mesh,
        in_specs=(
            P("asset", "seq", None),
            P(),
            P(),
            P(),
            P("asset", None, "seq"),
            P("asset"),
            P(),
            P(),
            P("asset", None, "seq", None),
            P("asset", None, None),
        ),
        out_specs=(P("asset", "seq", None), P("asset", None, "seq", None)),
        check_vma=False,
    )
```
